256 devices in a mesh: wide: 16 (over z, core), narrow: 16 (over y, x).
Axes of the slice: x: 4, y: 4, z: 8, core: 2. Of those that a mesh axis runs over, the one named last changes fastest.
Arguments:
- histories: bfloat16 [16, 16, 1024, 256], P('wide', 'narrow')
- lengths: int32 [16, 16, 4], P('wide', 'narrow'), may hold values from 0 to 1024, as said below
- w_in: bfloat16 [256, 1024], replicated, may hold values from -0.375 to 0.375
- w_out: bfloat16 [256, 256], replicated, may hold values from -0.375 to 0.375
- item_table: float32 [524288, 256], P(('wide', 'narrow'))
- neg_blocks: int32 [16, 64], P('wide'), may hold values from 0 to 4095, as said below
- targets: int32 [16, 16, 512], P('wide'), may hold values from 0 to 524287, as said below
Outputs:
- losses: float32 [16, 16, 512], P('wide', 'narrow')
- item_grad: float32 [524288, 256], P(('wide', 'narrow'))
The draws below stay inside these ranges and needn't reach their ends.
Inputs may be any that keep to these rules, and one draw needn't show every extreme that they name: Each device's lengths sum to at most 1024; the sums of the 16 devices with one narrow index add up to 16 * 512, and one of them is exactly 1024; some device holds one history of exactly 1024 slots. `neg_blocks`: row w lists 64 distinct blocks, each held by a device of wide index w (block b is item rows b * 128 to b * 128 + 127, held by device b // 16 of wide+narrow), exactly 64 // 16 from each such device. targets[w, n, j] is an item row of one of the blocks in neg_blocks[w].
All inputs are finite; a program needn't handle non-finite values.
Results may differ from the reference program's by a relative error of at most 0.0043.
Values may be sent and summed in bfloat16 or wider, within the bound.
A program may use at most 128 MiB of HBM per device.

```python
import math
import jax
import jax.numpy as jnp
from jax import lax

D = 256
HEADS = 2
DH = 128
QK = 256
BLOCK = 128
TOK_BAL = 512
CAP = 1024
SEQ_DEV = 4
NB = 64
BLKS_DEV = 16
ITEMS = 524288
N_WIDE = 16
N_NARROW = 16


def neg_layout(key):
    per_owner = NB // N_NARROW
    owner_keys = jax.random.split(jax.random.fold_in(key, 101), N_WIDE * N_NARROW)
    order_keys = jax.random.split(jax.random.fold_in(key, 202), N_WIDE)
    picked = jax.vmap(lambda one_key: jax.random.permutation(one_key, BLKS_DEV)[:per_owner])(owner_keys)
    owners = jnp.arange(N_WIDE * N_NARROW, dtype=jnp.int32)[:, None] * BLKS_DEV
    blocks = (picked.astype(jnp.int32) + owners).reshape(N_WIDE, NB)
    return jax.vmap(lambda one_key, row: jax.random.permutation(one_key, row))(order_keys, blocks).astype(jnp.int32)


def length_layout(key):
    key = jax.random.fold_in(key, 3)
    pair_key, cut_key = jax.random.split(key)

    def one_group(group_key):
        perm_key, size_key = jax.random.split(group_key)
        order = jax.random.permutation(perm_key, N_WIDE)
        moved = jax.random.randint(size_key, (N_WIDE // 2,), 0, TOK_BAL + 1).astype(jnp.int32)
        moved = moved.at[0].set(TOK_BAL)
        sums = jnp.zeros((N_WIDE,), jnp.int32)
        sums = sums.at[order[0::2]].set(TOK_BAL + moved)
        return sums.at[order[1::2]].set(TOK_BAL - moved)
    sums = jax.vmap(one_group)(jax.random.split(pair_key, N_NARROW)).T
    cuts = jax.random.randint(cut_key, (N_WIDE, N_NARROW, SEQ_DEV - 1), 0, sums[:, :, None] + 1).astype(jnp.int32)
    cuts = jnp.sort(cuts, axis=-1)
    cuts = jnp.where(sums[:, :, None] == 2 * TOK_BAL, 0, cuts).astype(jnp.int32)
    edges = jnp.concatenate([jnp.zeros((N_WIDE, N_NARROW, 1), jnp.int32), cuts, sums[:, :, None]], axis=-1)
    return (edges[..., 1:] - edges[..., :-1]).astype(jnp.int32)


def draw_neg_blocks(key, part):
    blocks = neg_layout(key)
    return blocks


def draw_targets(key, part):
    blocks = neg_layout(key)
    key = jax.random.fold_in(key, 7)
    pick_key, offset_key = jax.random.split(key)
    picks = jax.random.randint(pick_key, (N_WIDE, N_NARROW, TOK_BAL), 0, NB)
    offsets = jax.random.randint(offset_key, (N_WIDE, N_NARROW, TOK_BAL), 0, BLOCK)
    chosen = blocks[jnp.arange(N_WIDE)[:, None, None], picks]
    return (chosen * BLOCK + offsets).astype(jnp.int32)


def draw_lengths(key, part):
    return length_layout(key)


def draw_histories(key, part):
    lengths = length_layout(key)
    key = jax.random.fold_in(key, 11)
    base_key = jax.random.fold_in(key, 0)
    row_key = jax.random.fold_in(key, 1)
    col_key = jax.random.fold_in(key, 2)
    quiet_key = jax.random.fold_in(key, 4)
    shape = (N_WIDE, N_NARROW, CAP, D)
    base = jax.random.normal(base_key, shape, jnp.float32)
    low, high = (math.log(0.5), math.log(5.0))
    rows = jnp.exp(jax.random.uniform(row_key, (N_WIDE, N_NARROW, CAP, 1), jnp.float32, low, high))
    cols = jnp.exp(jax.random.uniform(col_key, (D,), jnp.float32, math.log(0.5), math.log(2.0)))
    totals = jnp.sum(lengths, axis=-1).astype(jnp.int32)
    chosen = jax.random.randint(quiet_key, (N_WIDE, N_NARROW), 0, 2).astype(jnp.int32) == 1
    slot_ids = jnp.arange(CAP, dtype=jnp.int32)
    silent = chosen[:, :, None] & (totals[:, :, None] > 0) & (slot_ids[None, None, :] == totals[:, :, None] - 1)
    keep = jnp.where(silent, 0.0, 1.0).astype(jnp.float32)[..., None]
    return (base * rows * cols * keep).astype(jnp.bfloat16)


def draw_item_table(key, part):
    key = jax.random.fold_in(key, 13)
    base_key = jax.random.fold_in(key, 0)
    row_key = jax.random.fold_in(key, 1)
    col_key = jax.random.fold_in(key, 2)
    centre_key = jax.random.fold_in(key, 4)
    assign_key = jax.random.fold_in(key, 5)
    weight_key = jax.random.fold_in(key, 6)
    base = jax.random.normal(base_key, (ITEMS, D), jnp.float32)
    low, high = (math.log(0.3), math.log(3.0))
    centre_weight = jnp.exp(jax.random.uniform(weight_key, (16, 1), jnp.float32, math.log(2.0), math.log(4.5)))
    centres = jax.random.normal(centre_key, (16, D), jnp.float32) * centre_weight
    assign = jax.random.randint(assign_key, (ITEMS,), 0, 16).astype(jnp.int32)
    shifted = base + jnp.take(centres, assign, axis=0)
    rows = jnp.exp(jax.random.uniform(row_key, (ITEMS, 1), jnp.float32, low, high))
    cols = jnp.exp(jax.random.uniform(col_key, (D,), jnp.float32, math.log(0.5), math.log(2.0)))
    return shifted * rows * cols


def noise(key, dims, deviation, reach, held_as=jnp.bfloat16):
    values = deviation * jax.random.normal(key, dims, jnp.float32)
    return jnp.clip(values, min=-reach, max=reach).astype(held_as)


def setup_inputs(seed: int = 0) -> dict:
    splits = jax.random.split(jax.random.key(seed), 8)
    return {
        "histories": draw_histories(jax.random.fold_in(splits[7], 71), 0),
        "lengths": draw_lengths(jax.random.fold_in(splits[7], 71), 0),
        "w_in": noise(splits[2], (D, 4 * QK), D ** -0.5, 0.375),
        "w_out": noise(splits[3], (QK, D), QK ** -0.5, 0.375),
        "item_table": draw_item_table(jax.random.fold_in(splits[7], 71), 0),
        "neg_blocks": draw_neg_blocks(jax.random.fold_in(splits[7], 71), 0),
        "targets": draw_targets(jax.random.fold_in(splits[7], 71), 0),
    }


logit_scale = 20.0

def unit_rows(rows):
    return rows * lax.rsqrt(lax.optimization_barrier(jnp.mean(rows * rows, axis=-1, keepdims=True)) + 1e-06) * rows.shape[-1] ** (-0.5)

def encode(history, lengths_dev, w_in, w_out):
    slots = history.shape[0]
    width = w_out.shape[0]
    projected = jax.nn.silu(jnp.dot(history, w_in, preferred_element_type=jnp.float32)).astype(jnp.bfloat16)
    gate_u = projected[:, :width]
    values = projected[:, width:2 * width].reshape(slots, HEADS, DH)
    query = projected[:, 2 * width:3 * width].reshape(slots, HEADS, DH)
    keys_h = projected[:, 3 * width:].reshape(slots, HEADS, DH)
    places = jnp.arange(slots, dtype=jnp.int32)
    ends = jnp.cumsum(lengths_dev).astype(jnp.int32)
    segment = lax.optimization_barrier(jnp.sum((places[:, None] >= ends[None, :]).astype(jnp.int32), axis=1))
    seq_start = lax.optimization_barrier(jnp.max(jnp.where(ends[None, :] <= places[:, None], ends[None, :], 0), axis=1))
    counts = (places - seq_start + 1).astype(jnp.float32)
    allowed = (segment[:, None] == segment[None, :]) & (places[None, :] <= places[:, None])
    scores = jnp.einsum('ihd,jhd->hij', query.astype(jnp.float32), keys_h.astype(jnp.float32))
    weights = jnp.where(allowed[None], jax.nn.silu(scores * DH ** (-0.5)), 0.0) / counts[None, :, None]
    weights = weights.astype(jnp.bfloat16)
    attended = jnp.einsum('hij,jhd->ihd', weights.astype(jnp.float32), values.astype(jnp.float32)).reshape(slots, width)
    average = lax.optimization_barrier(jnp.mean(attended, axis=-1, keepdims=True))
    spread = lax.optimization_barrier(jnp.mean((attended - average) ** 2, axis=-1, keepdims=True))
    mixed = ((attended - average) * lax.rsqrt(spread + 1e-05) * gate_u.astype(jnp.float32)).astype(jnp.bfloat16)
    state = history.astype(jnp.float32) + jnp.dot(mixed, w_out, preferred_element_type=jnp.float32)
    live = places < ends[-1]
    return jnp.where(live[:, None], unit_rows(state), 0.0).astype(jnp.bfloat16)

def reference(histories, lengths, w_in, w_out, item_table, neg_blocks, targets):
    flat_hist = histories.reshape(N_WIDE * N_NARROW, CAP, D)
    flat_len = lengths.reshape(N_WIDE * N_NARROW, SEQ_DEV)
    encoded = lax.map(lambda pair: encode(pair[0], pair[1], w_in, w_out), (flat_hist, flat_len))
    encoded = encoded.reshape(N_WIDE, N_NARROW, CAP, D)
    totals = lax.optimization_barrier(jnp.sum(lengths, axis=2)).astype(jnp.int32)
    ends = jnp.cumsum(totals, axis=0).astype(jnp.int32)
    starts = ends - totals
    stream_pos = jnp.arange(TOK_BAL, dtype=jnp.int32)[None, :] * N_WIDE + jnp.arange(N_WIDE, dtype=jnp.int32)[:, None]
    source = lax.optimization_barrier(jnp.sum((ends[None, None, :, :] <= stream_pos[:, :, None, None]).astype(jnp.int32), axis=2))
    narrow_idx = jnp.arange(N_NARROW, dtype=jnp.int32)[None, None, :]
    inner = stream_pos[:, :, None] - starts[source, narrow_idx]
    balanced = jnp.transpose(encoded[source, narrow_idx, inner], (0, 2, 1, 3))
    block_rows = jnp.arange(BLOCK, dtype=jnp.int32)

    def group(inputs):
        blocks, group_hb, group_targets = inputs
        item_ids = (blocks[:, None] * BLOCK + block_rows[None, :]).reshape(-1).astype(jnp.int32)
        raw = item_table[item_ids]
        cand_unit = unit_rows(raw).astype(jnp.bfloat16)

        def one_device(total, pair):
            token_rows, token_targets = pair
            logits = logit_scale * jnp.dot(token_rows, cand_unit.T, preferred_element_type=jnp.float32)
            hit = item_ids[None, :] == token_targets[:, None]
            sumexp = lax.optimization_barrier(jnp.sum(jnp.exp(logits), axis=1))
            loss = jnp.log(sumexp) - lax.optimization_barrier(jnp.sum(jnp.where(hit, logits, 0.0), axis=1))
            slope = (jnp.exp(logits) / sumexp[:, None] - hit.astype(jnp.float32)).astype(jnp.bfloat16)
            return (total + logit_scale * jnp.dot(slope.T, token_rows, preferred_element_type=jnp.float32), loss)
        grads, loss_rows = lax.scan(one_device, jnp.zeros((NB * BLOCK, D), jnp.float32), (group_hb, group_targets))
        _, pull = jax.vjp(unit_rows, raw)
        return (pull(grads)[0], item_ids, loss_rows)
    row_grads, all_ids, losses = lax.map(group, (neg_blocks, balanced, targets))
    item_grad = jnp.zeros((ITEMS, D), jnp.float32).at[all_ids.reshape(-1)].set(row_grads.reshape(-1, D))
    return (losses, item_grad)
```

```python
import math

import jax
import jax.numpy as jnp
from jax import lax
from jax.experimental import pallas as pl
from jax.experimental.pallas import tpu as pltpu
from jax.sharding import PartitionSpec as P

D = 256
DH = 128
BLOCK = 128
GROUP = 16
SIDE = 4
SLOTS = 1024
TILE = 256
TILES = SLOTS // TILE
PART = TILE // GROUP
PAIR = SLOTS // GROUP
TOK = 512
CAND = 512
SCALE = 20.0
MESH = pl.DeviceIdType.MESH
F32 = jnp.float32
BF16 = jnp.bfloat16


def unit_scale(rows):
    return lax.rsqrt(jnp.mean(rows * rows, axis=-1, keepdims=True) + 1e-06)


def silu(x):
    half = 0.5 * x
    return half + half * jnp.tanh(half)


def prep_kernel(neg_ref, table_ref, units_ref, raw_ref, order_ref, counts, sems):
    wide = lax.axis_index("wide")
    narrow = lax.axis_index("narrow")
    for owner in range(GROUP):
        counts[owner] = 0

    @pl.loop(0, 64)
    def _(i):
        block = neg_ref[0, i]
        owner = lax.shift_right_logical(block, 4) - wide * GROUP
        seen = counts[owner]
        order_ref[owner * 4 + seen] = block
        counts[owner] = seen + 1

    first = (wide * GROUP + narrow) * 16
    copies = []
    for q in range(4):
        row = pl.multiple_of((order_ref[narrow * 4 + q] - first) * BLOCK, BLOCK)
        copy = pltpu.make_async_copy(
            table_ref.at[pl.ds(row, BLOCK)], raw_ref.at[pl.ds(q * BLOCK, BLOCK)], sems.at[q]
        )
        copy.start()
        copies.append(copy)
    for q in range(4):
        copies[q].wait()
        rows = raw_ref[pl.ds(q * BLOCK, BLOCK), :]
        units_ref[pl.ds(q * BLOCK, BLOCK), :] = (rows * unit_scale(rows) * 0.0625).astype(BF16)


def prep(neg_blocks, item_table):
    return pl.pallas_call(
        prep_kernel,
        out_shape=(
            jax.ShapeDtypeStruct((CAND, D), BF16),
            jax.ShapeDtypeStruct((CAND, D), F32),
            jax.ShapeDtypeStruct((64,), jnp.int32),
        ),
        in_specs=[pl.BlockSpec(memory_space=pltpu.SMEM), pl.BlockSpec(memory_space=pl.ANY)],
        out_specs=(
            pl.BlockSpec(memory_space=pltpu.VMEM),
            pl.BlockSpec(memory_space=pltpu.VMEM),
            pl.BlockSpec(memory_space=pltpu.SMEM),
        ),
        scratch_shapes=[pltpu.SMEM((GROUP,), jnp.int32), pltpu.SemaphoreType.DMA((4,))],
        compiler_params=pltpu.CompilerParams(vmem_limit_bytes=16 * 2**20),
        name="prep",
    )(neg_blocks, item_table)


def main_kernel(
    len_ref,
    order_ref,
    hist_ref,
    win_ref,
    wout_ref,
    units_ref,
    targets_ref,
    grad_ref,
    loss_ref,
    proj,
    tot,
    send,
    recv,
    tok,
    cand,
    expd,
    slope,
    sums,
    hits,
    gsend,
    grecv,
    tot_s,
    tot_r,
    a2a_s,
    a2a_r,
    cand_s,
    cand_r,
    tok_s,
    tok_r,
    sum_s,
    sum_r,
    hit_s,
    hit_r,
    g_s,
    g_r,
):
    me = lax.axis_index("wide")
    narrow = lax.axis_index("narrow")
    core = lax.rem(me, 2)
    tok_step = 4 - 3 * core
    cand_step = 1 + 3 * core
    my_t = lax.rem(narrow // tok_step, SIDE)
    my_c = lax.rem(narrow // cand_step, SIDE)

    def wide_peer(d):
        return (lax.rem(me + d, GROUP), narrow)

    def tok_peer(s):
        return (me, lax.rem(my_t + s, SIDE) * tok_step + my_c * cand_step)

    def cand_peer(s):
        return (me, my_t * tok_step + lax.rem(my_c + s, SIDE) * cand_step)

    def remote(src, dst, ssem, rsem, peer):
        return pltpu.make_async_remote_copy(
            src_ref=src, dst_ref=dst, send_sem=ssem, recv_sem=rsem, device_id=peer, device_id_type=MESH
        )

    barrier = pltpu.get_barrier_semaphore()
    for d in range(1, GROUP):
        pl.semaphore_signal(barrier, inc=1, device_id=wide_peer(d), device_id_type=MESH)
    for s in range(1, SIDE):
        pl.semaphore_signal(barrier, inc=1, device_id=tok_peer(s), device_id_type=MESH)
        pl.semaphore_signal(barrier, inc=1, device_id=cand_peer(s), device_id_type=MESH)

    e0 = len_ref[0, 0, 0]
    e1 = e0 + len_ref[0, 0, 1]
    e2 = e1 + len_ref[0, 0, 2]
    e3 = e2 + len_ref[0, 0, 3]
    tot[me] = jnp.full((8, 128), e3, jnp.int32)
    cand[my_c] = units_ref[...]
    pl.semaphore_wait(barrier, GROUP - 1 + 2 * (SIDE - 1))

    tot_copies = [remote(tot.at[me], tot.at[me], tot_s.at[d], tot_r.at[d], wide_peer(d)) for d in range(1, GROUP)]
    for copy in tot_copies:
        copy.start()
    cand_copies = [
        remote(units_ref, cand.at[my_c], cand_s.at[s], cand_r.at[s], cand_peer(s)) for s in range(1, SIDE)
    ]
    for copy in cand_copies:
        copy.start()

    for b in range(TILES):
        rows = pl.ds(b * TILE, TILE)
        x = jnp.dot(hist_ref[0, 0, rows, :], win_ref[...], preferred_element_type=F32)
        proj[rows, :] = silu(x).astype(BF16)

    lanes = lax.broadcasted_iota(jnp.int32, (TILE, TILE), 1)
    subs = lax.broadcasted_iota(jnp.int32, (TILE, TILE), 0)
    take = None
    for b in range(TILES):
        rows = pl.ds(b * TILE, TILE)
        place = subs + b * TILE
        start = jnp.maximum(
            jnp.maximum(jnp.where(place >= e0, e0, 0), jnp.where(place >= e1, e1, 0)),
            jnp.maximum(jnp.where(place >= e2, e2, 0), jnp.where(place >= e3, e3, 0)),
        )
        share = 1.0 / (place - start + 1).astype(F32)
        heads = []
        for h in range(2):
            q = proj[rows, pl.ds(512 + h * DH, DH)]
            total = jnp.zeros((TILE, DH), F32)
            for kb in range(b + 1):
                krows = pl.ds(kb * TILE, TILE)
                k = proj[krows, pl.ds(768 + h * DH, DH)]
                v = proj[krows, pl.ds(256 + h * DH, DH)]
                scores = lax.dot_general(q, k, (((1,), (1,)), ((), ())), preferred_element_type=F32)
                weights = silu(scores * (DH ** -0.5)) * share
                allowed = lanes + kb * TILE >= start
                if kb == b:
                    allowed = allowed & (lanes <= subs)
                weights = jnp.where(allowed, weights, 0.0).astype(BF16)
                total = total + jnp.dot(weights, v, preferred_element_type=F32)
            heads.append(total)
        attended = jnp.concatenate(heads, axis=1)
        centred = attended - jnp.mean(attended, axis=-1, keepdims=True)
        spread = jnp.mean(centred * centred, axis=-1, keepdims=True)
        gate = proj[rows, pl.ds(0, D)].astype(F32)
        mixed = (centred * lax.rsqrt(spread + 1e-05) * gate).astype(BF16)
        state = hist_ref[0, 0, rows, :].astype(F32) + jnp.dot(mixed, wout_ref[...], preferred_element_type=F32)
        encoded = jnp.where(place < e3, state * unit_scale(state) * 0.0625, 0.0).astype(BF16)
        if b == 0:
            for copy in tot_copies:
                copy.wait_recv()
            begin = jnp.zeros((8, 128), jnp.int32)
            for w in range(GROUP):
                begin = begin + jnp.where(w < me, tot[w], 0)
            begin = jnp.concatenate([begin[0:1, :]] * 2, axis=1)
            wanted = (subs & 15) * 16 + (((subs >> 4) - begin) & 15)
            take = (lanes == wanted).astype(F32).astype(BF16)
        packed = jnp.dot(take, encoded, preferred_element_type=F32).astype(BF16)
        send[b] = packed.reshape(GROUP, PART, D)
        for d in range(1, GROUP):
            dest = lax.rem(me + d, GROUP)
            remote(
                send.at[b, dest], recv.at[me, pl.ds(b * PART, PART)], a2a_s, a2a_r, wide_peer(d)
            ).start()
        recv[me, pl.ds(b * PART, PART), :] = send[b, me]

    pltpu.make_async_copy(recv.at[pl.ds(0, GROUP - 1)], recv.at[pl.ds(0, GROUP - 1)], a2a_r).wait()
    lane = lax.broadcasted_iota(jnp.int32, (1, 128), 1)
    slot = lax.broadcasted_iota(jnp.int32, (TOK, 128), 0)
    begin = jnp.zeros((1, 128), jnp.int32)
    pieces = []
    for w in range(0, GROUP, 2):
        second = begin + tot[w, 0:1, :]
        base = jnp.where(lane < PAIR, begin, second)
        goes_to = ((base - me + 15) >> 4) + (lane & (PAIR - 1))
        pieces.append((slot == goes_to).astype(F32).astype(BF16))
        begin = second + tot[w + 1, 0:1, :]
    gather = jnp.concatenate(pieces, axis=1)
    tok[my_t] = jnp.dot(gather, recv[...].reshape(GROUP * PAIR, D), preferred_element_type=F32).astype(BF16)

    tok_copies = [
        remote(tok.at[my_t], tok.at[my_t], tok_s.at[s], tok_r.at[s], tok_peer(s)) for s in range(1, SIDE)
    ]
    for copy in tok_copies:
        copy.start()
    for copy in cand_copies:
        copy.wait_recv()

    row8 = lax.broadcasted_iota(jnp.int32, (8, TOK), 0)
    part = jnp.zeros((8, TOK), F32)
    for s in (0, 1, 3, 2):
        if s:
            tok_copies[s - 1].wait_recv()
        t = lax.rem(my_t + SIDE - s, SIDE)

        def forward(c, total):
            scores = lax.dot_general(
                cand[c], tok[t], (((1,), (1,)), ((), ())), preferred_element_type=F32
            )
            value = jnp.exp2(scores * (SCALE * math.log2(math.e)))
            expd[t, pl.ds(pl.multiple_of(c * CAND, CAND), CAND), :] = value
            return total + jnp.sum(value.reshape(CAND // 8, 8, TOK), axis=0)

        total = lax.fori_loop(0, SIDE, forward, jnp.zeros((8, TOK), F32))
        part = jnp.where(row8 == t, jnp.sum(total, axis=0, keepdims=True), part)
    sums[my_t] = part
    sum_copies = [
        remote(sums.at[my_t], sums.at[my_t], sum_s.at[s], sum_r.at[s], tok_peer(s)) for s in range(1, SIDE)
    ]
    for copy in sum_copies:
        copy.start()
    for copy in sum_copies:
        copy.wait_recv()
    sumexp = (sums[0] + sums[1]) + (sums[2] + sums[3])
    inverse = 1.0 / sumexp

    offset = lax.broadcasted_iota(jnp.int32, (BLOCK, TOK), 0)
    hit_part = jnp.zeros((8, TOK), F32)
    g_copies = []
    own = None
    for s in (1, 3, 2, 0):
        c = lax.rem(my_c + s, SIDE)
        owner = my_t * tok_step + c * cand_step
        for t in range(SIDE):
            target = targets_ref[0, pl.ds(t * tok_step + my_c * cand_step, 1), :]
            scale_t = inverse[t : t + 1, :]

            def backward(q, total):
                at = pl.multiple_of(c * CAND + q * BLOCK, BLOCK)
                value = expd[t, pl.ds(at, BLOCK), :]
                hit = offset == target - order_ref[owner * 4 + q] * BLOCK
                grad = value * scale_t - jnp.where(hit, 1.0, 0.0)
                slope[pl.ds(pl.multiple_of(q * BLOCK, BLOCK), BLOCK), pl.ds(t * TOK, TOK)] = grad.astype(BF16)
                found = jnp.where(hit, value, 0.0)
                return total + jnp.sum(found.reshape(BLOCK // 8, 8, TOK), axis=0)

            found = lax.fori_loop(0, 4, backward, jnp.zeros((8, TOK), F32))
            hit_part = hit_part + jnp.where(row8 == t, jnp.sum(found, axis=0, keepdims=True), 0.0)
        grads = SCALE * jnp.dot(slope[...], tok[...].reshape(SIDE * TOK, D), preferred_element_type=F32)
        if s:
            gsend[s] = grads.astype(BF16)
            copy = remote(gsend.at[s], grecv.at[s], g_s.at[s], g_r.at[s], cand_peer(s))
            copy.start()
            g_copies.append(copy)
        else:
            grad_ref[...] = grads
    hits[my_t] = hit_part
    hit_copies = [
        remote(hits.at[my_t], hits.at[my_t], hit_s.at[s], hit_r.at[s], tok_peer(s)) for s in range(1, SIDE)
    ]
    for copy in hit_copies:
        copy.start()
    for copy in hit_copies:
        copy.wait_recv()
    found = (hits[0] + hits[1]) + (hits[2] + hits[3])
    loss = jnp.where(row8 == my_t, jnp.log(sumexp) - jnp.log(found), 0.0)
    loss_ref[...] = jnp.sum(loss, axis=0, keepdims=True)
    for copy in g_copies:
        copy.wait_recv()
    grad_ref[...] += (grecv[1].astype(F32) + grecv[2].astype(F32)) + grecv[3].astype(F32)

    for copy in tot_copies + cand_copies + tok_copies + sum_copies + hit_copies + g_copies:
        copy.wait_send()
    pltpu.make_async_copy(recv.at[pl.ds(0, GROUP - 1)], recv.at[pl.ds(0, GROUP - 1)], a2a_s).wait()


def main(lengths, order, histories, w_in, w_out, units, targets):
    dma = pltpu.SemaphoreType.DMA
    vmem = pl.BlockSpec(memory_space=pltpu.VMEM)
    smem = pl.BlockSpec(memory_space=pltpu.SMEM)
    return pl.pallas_call(
        main_kernel,
        out_shape=(jax.ShapeDtypeStruct((CAND, D), F32), jax.ShapeDtypeStruct((1, TOK), F32)),
        in_specs=[smem, smem, vmem, vmem, vmem, vmem, vmem],
        out_specs=(vmem, vmem),
        scratch_shapes=[
            pltpu.VMEM((SLOTS, 4 * D), BF16),
            pltpu.VMEM((GROUP, 8, 128), jnp.int32),
            pltpu.VMEM((TILES, GROUP, PART, D), BF16),
            pltpu.VMEM((GROUP, PAIR, D), BF16),
            pltpu.VMEM((SIDE, TOK, D), BF16),
            pltpu.VMEM((SIDE, CAND, D), BF16),
            pltpu.VMEM((SIDE, SIDE * CAND, TOK), F32),
            pltpu.VMEM((CAND, SIDE * TOK), BF16),
            pltpu.VMEM((SIDE, 8, TOK), F32),
            pltpu.VMEM((SIDE, 8, TOK), F32),
            pltpu.VMEM((SIDE, CAND, D), BF16),
            pltpu.VMEM((SIDE, CAND, D), BF16),
            dma((GROUP,)),
            dma((GROUP,)),
            dma,
            dma,
        ]
        + [dma((SIDE,))] * 10,
        compiler_params=pltpu.CompilerParams(
            collective_id=0, has_side_effects=True, vmem_limit_bytes=48 * 2**20
        ),
        name="main",
    )(lengths, order, histories, w_in, w_out, units, targets)


def finish_kernel(order_ref, grad_ref, raw_ref, loss_in, out_ref, loss_ref):
    wide = lax.axis_index("wide")
    narrow = lax.axis_index("narrow")
    first = (wide * GROUP + narrow) * 16
    loss_ref[...] = loss_in[...]
    out_ref[...] = jnp.zeros_like(out_ref)
    for q in range(4):
        rows = raw_ref[pl.ds(q * BLOCK, BLOCK), :]
        grad = grad_ref[pl.ds(q * BLOCK, BLOCK), :]
        scale = unit_scale(rows)
        along = jnp.mean(rows * grad, axis=-1, keepdims=True)
        value = (grad - rows * (scale * scale * along)) * (scale * 0.0625)
        at = pl.multiple_of((order_ref[narrow * 4 + q] - first) * BLOCK, BLOCK)
        out_ref[pl.ds(at, BLOCK), :] = value


def finish(order, grads, raw, loss):
    vmem = pl.BlockSpec(memory_space=pltpu.VMEM)
    return pl.pallas_call(
        finish_kernel,
        out_shape=(jax.ShapeDtypeStruct((16 * BLOCK, D), F32), jax.ShapeDtypeStruct((1, TOK), F32)),
        in_specs=[pl.BlockSpec(memory_space=pltpu.SMEM), vmem, vmem, vmem],
        out_specs=(vmem, vmem),
        compiler_params=pltpu.CompilerParams(vmem_limit_bytes=16 * 2**20),
        name="finish",
    )(order, grads, raw, loss)


def local(histories, lengths, w_in, w_out, item_table, neg_blocks, targets):
    units, raw, order = prep(neg_blocks, item_table)
    grads, loss = main(lengths, order, histories, w_in, w_out, units, targets)
    item_grad, loss = finish(order, grads, raw, loss)
    return (loss[None], item_grad)


def solution(mesh):
    in_specs = (
        P("wide", "narrow", None, None),
        P("wide", "narrow", None),
        P(),
        P(),
        P(("wide", "narrow"), None),
        P("wide", None),
        P("wide", None, None),
    )
    out_specs = (P("wide", "narrow", None), P(("wide", "narrow"), None))
    return jax.shard_map(local, mesh=mesh, in_specs=in_specs, out_specs=out_specs, check_vma=False)
```

```python
import math

import jax
import jax.numpy as jnp
from jax import lax
from jax.experimental import pallas as pl
from jax.experimental.pallas import tpu as pltpu
from jax.sharding import PartitionSpec as P

D = 256
DH = 128
BLOCK = 128
GROUP = 16
SIDE = 4
SLOTS = 1024
TILE = 256
TILES = SLOTS // TILE
PART = TILE // GROUP
PAIR = SLOTS // GROUP
TOK = 512
CAND = 512
SCALE = 20.0
EARLY = 2
ARRIVE = (1, 3, 2)
HALF = TOK // 2
FAR_FIRST = (8, 9, 7, 10, 6, 11, 5, 12, 4, 13, 3, 14, 2, 15, 1)
MESH = pl.DeviceIdType.MESH
F32 = jnp.float32
BF16 = jnp.bfloat16


def unit_scale(rows):
    return lax.rsqrt(jnp.mean(rows * rows, axis=-1, keepdims=True) + 1e-06)


def silu(x):
    half = 0.5 * x
    return half + half * jnp.tanh(half)


def main_kernel(
    len_ref,
    neg_ref,
    hist_ref,
    win_ref,
    wout_ref,
    table_ref,
    targets_ref,
    grad_ref,
    loss_ref,
    own_ref,
    proj,
    enc,
    tot,
    units,
    send,
    recv,
    tok,
    cand,
    expd,
    sums,
    gsend,
    grecv,
    hits,
    raw_ref,
    tot_s,
    tot_r,
    a2a_s,
    a2a_r,
    cand_s,
    cand_r,
    tok_s,
    tok_r,
    sum_s,
    sum_r,
    hit_s,
    hit_r,
    g_s,
    g_r,
):
    me = lax.axis_index("wide")
    narrow = lax.axis_index("narrow")
    core = lax.rem(me, 2)
    tok_step = 4 - 3 * core
    cand_step = 1 + 3 * core
    my_t = lax.rem(narrow // tok_step, SIDE)
    my_c = lax.rem(narrow // cand_step, SIDE)

    def wide_peer(d):
        return (lax.rem(me + d, GROUP), narrow)

    def tok_peer(s):
        return (me, lax.rem(my_t + s, SIDE) * tok_step + my_c * cand_step)

    def cand_peer(s):
        return (me, my_t * tok_step + lax.rem(my_c + s, SIDE) * cand_step)

    def remote(src, dst, ssem, rsem, peer):
        return pltpu.make_async_remote_copy(
            src_ref=src, dst_ref=dst, send_sem=ssem, recv_sem=rsem, device_id=peer, device_id_type=MESH
        )

    barrier = pltpu.get_barrier_semaphore()
    for d in FAR_FIRST:
        pl.semaphore_signal(barrier, inc=1, device_id=wide_peer(d), device_id_type=MESH)
    for s in range(1, SIDE):
        pl.semaphore_signal(barrier, inc=1, device_id=tok_peer(s), device_id_type=MESH)
        pl.semaphore_signal(barrier, inc=1, device_id=cand_peer(s), device_id_type=MESH)

    e0 = len_ref[0, 0, 0]
    e1 = e0 + len_ref[0, 0, 1]
    e2 = e1 + len_ref[0, 0, 2]
    e3 = e2 + len_ref[0, 0, 3]
    tot[me] = jnp.full((8, 128), e3, jnp.int32)

    for b in range(TILES):
        rows = pl.ds(b * TILE, TILE)
        x = jnp.dot(hist_ref[0, 0, rows, :], win_ref[...], preferred_element_type=F32)
        proj[rows, :] = silu(x).astype(BF16)

    my_dev = me * GROUP + narrow
    blocks = [neg_ref[narrow * 4 + q] for q in range(4)]
    row8 = lax.broadcasted_iota(jnp.int32, (8, TOK), 0)
    row8s = row8[:, :128]
    held = jnp.zeros((8, 128), jnp.int32)
    for q in range(4):
        held = jnp.where(row8s == q, blocks[q], held)
    own_ref[...] = held * BLOCK
    own = [jnp.full((16, D), blocks[q] - my_dev * 16, jnp.int32) for q in range(4)]

    @pl.loop(0, BLOCK // 16)
    def _(i):
        at = pl.multiple_of(i * 16, 16)
        picked = [jnp.zeros((16, D), F32)] * 4
        for b in range(16):
            rows = table_ref[pl.ds(b * BLOCK + at, 16), :]
            picked = [jnp.where(own[q] == b, rows, picked[q]) for q in range(4)]
        for q in range(4):
            raw_ref[pl.ds(q * BLOCK + at, 16), :] = picked[q]

    rows = raw_ref[...]
    units[...] = (rows * unit_scale(rows) * 0.0625).astype(BF16)
    cand[my_c] = units[...]

    lanes = lax.broadcasted_iota(jnp.int32, (TILE, TILE), 1)
    subs = lax.broadcasted_iota(jnp.int32, (TILE, TILE), 0)

    def encode(b):
        rows = pl.ds(b * TILE, TILE)
        place = subs + b * TILE
        start = jnp.maximum(
            jnp.maximum(jnp.where(place >= e0, e0, 0), jnp.where(place >= e1, e1, 0)),
            jnp.maximum(jnp.where(place >= e2, e2, 0), jnp.where(place >= e3, e3, 0)),
        )
        share = 1.0 / (place - start + 1).astype(F32)
        heads = []
        for h in range(2):
            q = proj[rows, pl.ds(512 + h * DH, DH)]
            total = jnp.zeros((TILE, DH), F32)
            for kb in range(b + 1):
                krows = pl.ds(kb * TILE, TILE)
                k = proj[krows, pl.ds(768 + h * DH, DH)]
                v = proj[krows, pl.ds(256 + h * DH, DH)]
                scores = lax.dot_general(q, k, (((1,), (1,)), ((), ())), preferred_element_type=F32)
                weights = silu(scores * (DH ** -0.5)) * share
                allowed = lanes + kb * TILE >= start
                if kb == b:
                    allowed = allowed & (lanes <= subs)
                weights = jnp.where(allowed, weights, 0.0).astype(BF16)
                total = total + jnp.dot(weights, v, preferred_element_type=F32)
            heads.append(total)
        attended = jnp.concatenate(heads, axis=1)
        centred = attended - jnp.mean(attended, axis=-1, keepdims=True)
        spread = jnp.mean(centred * centred, axis=-1, keepdims=True)
        gate = proj[rows, pl.ds(0, D)].astype(F32)
        mixed = (centred * lax.rsqrt(spread + 1e-05) * gate).astype(BF16)
        state = hist_ref[0, 0, rows, :].astype(F32) + jnp.dot(mixed, wout_ref[...], preferred_element_type=F32)
        enc[rows, :] = jnp.where(place < e3, state * unit_scale(state) * 0.0625, 0.0).astype(BF16)

    for b in range(EARLY):
        encode(b)

    pl.semaphore_wait(barrier, GROUP - 1 + 2 * (SIDE - 1))
    tot_copies = [remote(tot.at[me], tot.at[me], tot_s.at[d], tot_r.at[d], wide_peer(d)) for d in FAR_FIRST]
    cand_copies = [
        remote(units, cand.at[my_c], cand_s.at[s], cand_r.at[s], cand_peer(s)) for s in range(1, SIDE)
    ]
    for copy in tot_copies + cand_copies:
        copy.start()

    for b in range(EARLY, TILES):
        encode(b)

    for copy in tot_copies:
        copy.wait_recv()
    begin = jnp.zeros((8, 128), jnp.int32)
    for w in range(GROUP):
        begin = begin + jnp.where(w < me, tot[w], 0)
    begin = jnp.concatenate([begin[0:1, :]] * 2, axis=1)
    wanted = (subs & 15) * 16 + (((subs >> 4) - begin) & 15)
    take = (lanes == wanted).astype(F32).astype(BF16)
    for b in range(TILES):
        packed = jnp.dot(take, enc[pl.ds(b * TILE, TILE), :], preferred_element_type=F32).astype(BF16)
        send[b] = packed.reshape(GROUP, PART, D)
        for d in FAR_FIRST:
            dest = lax.rem(me + d, GROUP)
            remote(
                send.at[b, dest], recv.at[me, pl.ds(b * PART, PART)], a2a_s, a2a_r, wide_peer(d)
            ).start()
        recv[me, pl.ds(b * PART, PART), :] = send[b, me]

    lane = lax.broadcasted_iota(jnp.int32, (1, 128), 1)
    slot = lax.broadcasted_iota(jnp.int32, (TOK, 128), 0)
    begin = jnp.zeros((1, 128), jnp.int32)
    pieces = []
    for w in range(0, GROUP, 2):
        second = begin + tot[w, 0:1, :]
        base = jnp.where(lane < PAIR, begin, second)
        goes_to = ((base - me + 15) >> 4) + (lane & (PAIR - 1))
        pieces.append((slot == goes_to).astype(F32).astype(BF16))
        begin = second + tot[w + 1, 0:1, :]
    gather = jnp.concatenate(pieces, axis=1)
    pltpu.make_async_copy(recv.at[pl.ds(0, GROUP - 1)], recv.at[pl.ds(0, GROUP - 1)], a2a_r).wait()
    own_tok = jnp.dot(gather, recv[...].reshape(GROUP * PAIR, D), preferred_element_type=F32).astype(BF16)
    tok[my_t] = own_tok

    tok_copies = {
        s: remote(tok.at[my_t], tok.at[my_t], tok_s.at[s], tok_r.at[s], tok_peer(s)) for s in ARRIVE
    }
    for key in ARRIVE:
        tok_copies[key].start()
    for copy in cand_copies:
        copy.wait_recv()

    part = jnp.zeros((8, TOK), F32)
    for s in (0,) + ARRIVE:
        if s:
            tok_copies[s].wait_recv()
        t = lax.rem(my_t + SIDE - s, SIDE)

        def forward(c, total):
            scores = lax.dot_general(
                cand[c], tok[t], (((1,), (1,)), ((), ())), preferred_element_type=F32
            )
            value = jnp.exp2(scores * (SCALE * math.log2(math.e)))
            expd[t, pl.ds(pl.multiple_of(c * CAND, CAND), CAND), :] = value
            return total + jnp.sum(value.reshape(CAND // 8, 8, TOK), axis=0)

        total = lax.fori_loop(0, SIDE, forward, jnp.zeros((8, TOK), F32))
        part = jnp.where(row8 == t, jnp.sum(total, axis=0, keepdims=True), part)
    sums[my_t] = part
    sum_copies = [
        remote(sums.at[my_t], sums.at[my_t], sum_s.at[s], sum_r.at[s], tok_peer(s)) for s in range(1, SIDE)
    ]
    for s in (2, 1, 3):
        sum_copies[s - 1].start()

    offset = lax.broadcasted_iota(jnp.int32, (BLOCK, TOK), 0)

    def block_start(c, q):
        return neg_ref[(my_t * tok_step + c * cand_step) * 4 + q] * BLOCK

    def target_of(t):
        return targets_ref[0, pl.ds(t * tok_step + my_c * cand_step, 1), :]

    for copy in sum_copies:
        copy.wait_recv()
    sumexp = (sums[0] + sums[1]) + (sums[2] + sums[3])
    inverse = 1.0 / sumexp

    g_copies = []
    part = jnp.zeros((8, TOK), F32)
    for s in (2, 1, 3, 0):
        c = lax.rem(my_c + s, SIDE)
        for half in range(2):
            total = jnp.zeros((2 * BLOCK, D), F32)
            for t in range(SIDE):
                target = target_of(t)
                scale_t = inverse[t : t + 1, :]
                slopes = []
                found = jnp.zeros((8, TOK), F32)
                for q in (2 * half, 2 * half + 1):
                    value = expd[t, pl.ds(pl.multiple_of(c * CAND + q * BLOCK, BLOCK), BLOCK), :]
                    hit = offset == target - block_start(c, q)
                    slopes.append((value * scale_t - jnp.where(hit, 1.0, 0.0)).astype(BF16))
                    found = found + jnp.sum(jnp.where(hit, value, 0.0).reshape(BLOCK // 8, 8, TOK), axis=0)
                total = total + jnp.dot(jnp.concatenate(slopes, axis=0), tok[t], preferred_element_type=F32)
                part = part + jnp.where(row8 == t, jnp.sum(found, axis=0, keepdims=True), 0.0)
            rows = pl.ds(half * 2 * BLOCK, 2 * BLOCK)
            if s:
                gsend[s, rows, :] = (SCALE * total).astype(BF16)
            else:
                grad_ref[rows, :] = SCALE * total
        if s:
            copy = remote(gsend.at[s], grecv.at[s], g_s.at[s], g_r.at[s], cand_peer(s))
            copy.start()
            g_copies.append(copy)
    hits[my_t] = part
    hit_copies = [
        remote(hits.at[my_t], hits.at[my_t], hit_s.at[s], hit_r.at[s], tok_peer(s)) for s in range(1, SIDE)
    ]
    for s in (2, 1, 3):
        hit_copies[s - 1].start()
    for copy in hit_copies:
        copy.wait_recv()
    found = (hits[0] + hits[1]) + (hits[2] + hits[3])
    loss = jnp.where(row8 == my_t, jnp.log(sumexp) - jnp.log(found), 0.0)
    loss_ref[...] = jnp.sum(loss, axis=0, keepdims=True)
    for copy in g_copies:
        copy.wait_recv()
    for q in range(4):
        at = pl.ds(q * BLOCK, BLOCK)
        grad = (grad_ref[at, :] + grecv[1, at, :].astype(F32)) + (
            grecv[2, at, :].astype(F32) + grecv[3, at, :].astype(F32)
        )
        rows = raw_ref[at, :]
        scale = unit_scale(rows)
        along = jnp.mean(rows * grad, axis=-1, keepdims=True)
        grad_ref[at, :] = (grad - rows * (scale * scale * along)) * (scale * 0.0625)

    for copy in tot_copies + cand_copies + list(tok_copies.values()) + sum_copies + hit_copies + g_copies:
        copy.wait_send()
    pltpu.make_async_copy(recv.at[pl.ds(0, GROUP - 1)], recv.at[pl.ds(0, GROUP - 1)], a2a_s).wait()


def main(lengths, neg_blocks, histories, w_in, w_out, item_table, targets):
    dma = pltpu.SemaphoreType.DMA
    anywhere = pl.BlockSpec(memory_space=pl.ANY)
    vmem = pl.BlockSpec(memory_space=pltpu.VMEM)
    smem = pl.BlockSpec(memory_space=pltpu.SMEM)
    return pl.pallas_call(
        main_kernel,
        out_shape=(
            jax.ShapeDtypeStruct((CAND, D), F32),
            jax.ShapeDtypeStruct((1, TOK), F32),
            jax.ShapeDtypeStruct((8, 128), jnp.int32),
        ),
        in_specs=[smem, smem, vmem, vmem, vmem, vmem, vmem],
        out_specs=(vmem, vmem, vmem),
        scratch_shapes=[
            pltpu.VMEM((SLOTS, 4 * D), BF16),
            pltpu.VMEM((SLOTS, D), BF16),
            pltpu.VMEM((GROUP, 8, 128), jnp.int32),
            pltpu.VMEM((CAND, D), BF16),
            pltpu.VMEM((TILES, GROUP, PART, D), BF16),
            pltpu.VMEM((GROUP, PAIR, D), BF16),
            pltpu.VMEM((SIDE, TOK, D), BF16),
            pltpu.VMEM((SIDE, CAND, D), BF16),
            pltpu.VMEM((SIDE, SIDE * CAND, TOK), F32),
            pltpu.VMEM((SIDE, 8, TOK), F32),
            pltpu.VMEM((SIDE, CAND, D), BF16),
            pltpu.VMEM((SIDE, CAND, D), BF16),
            pltpu.VMEM((SIDE, 8, TOK), F32),
            pltpu.VMEM((CAND, D), F32),
            dma((GROUP,)),
            dma((GROUP,)),
            dma,
            dma,
        ]
        + [dma((SIDE,))] * 2
        + [dma((2 * SIDE,))] * 2
        + [dma((SIDE,))] * 4
        + [dma((2 * SIDE,))] * 2,
        compiler_params=pltpu.CompilerParams(
            collective_id=0, has_side_effects=True, vmem_limit_bytes=56 * 2**20
        ),
        name="main",
    )(lengths, neg_blocks, histories, w_in, w_out, item_table, targets)


def finish_kernel(own_hbm, value_hbm, loss_in, out_hbm, loss_hbm, zeros, value_ref, loss_ref, own_ref, in_s, out_s):
    first = (lax.axis_index("wide") * GROUP + lax.axis_index("narrow")) * 16 * BLOCK
    loads = [
        pltpu.make_async_copy(own_hbm, own_ref, in_s.at[0]),
        pltpu.make_async_copy(loss_in, loss_ref, in_s.at[1]),
        pltpu.make_async_copy(value_hbm, value_ref, in_s.at[2]),
    ]
    for load in loads:
        load.start()
    zeros[...] = jnp.zeros_like(zeros)
    blanks = [
        pltpu.make_async_copy(zeros, out_hbm.at[pl.ds(i * CAND, CAND)], out_s.at[i]) for i in range(4)
    ]
    for blank in blanks:
        blank.start()
    loads[1].wait()
    moves = [pltpu.make_async_copy(loss_ref, loss_hbm, out_s.at[8])]
    moves[0].start()
    loads[0].wait()
    loads[2].wait()
    for blank in blanks:
        blank.wait()
    for q in range(4):
        at = pl.multiple_of(own_ref[q, 0] - first, BLOCK)
        moves.append(
            pltpu.make_async_copy(
                value_ref.at[pl.ds(q * BLOCK, BLOCK)], out_hbm.at[pl.ds(at, BLOCK)], out_s.at[4 + q]
            )
        )
        moves[-1].start()
    for move in moves:
        move.wait()


def finish(own, value, loss):
    anywhere = pl.BlockSpec(memory_space=pl.ANY)
    return pl.pallas_call(
        finish_kernel,
        out_shape=(jax.ShapeDtypeStruct((16 * BLOCK, D), F32), jax.ShapeDtypeStruct((1, TOK), F32)),
        in_specs=[anywhere] * 3,
        out_specs=(anywhere, anywhere),
        scratch_shapes=[
            pltpu.VMEM((CAND, D), F32),
            pltpu.VMEM((CAND, D), F32),
            pltpu.VMEM((1, TOK), F32),
            pltpu.SMEM((8, 128), jnp.int32),
            pltpu.SemaphoreType.DMA((3,)),
            pltpu.SemaphoreType.DMA((9,)),
        ],
        compiler_params=pltpu.CompilerParams(vmem_limit_bytes=56 * 2**20),
        name="finish",
    )(own, value, loss)


def local(histories, lengths, w_in, w_out, item_table, neg_blocks, targets):
    blocks = neg_blocks[0]
    rank = jnp.sum((blocks[None, :] < blocks[:, None]).astype(jnp.int32), axis=1)
    places = jnp.arange(blocks.shape[0], dtype=jnp.int32)
    order = jnp.sum(jnp.where(rank[:, None] == places[None, :], blocks[:, None], 0), axis=0)
    value, loss, own = main(lengths, order, histories, w_in, w_out, item_table, targets)
    item_grad, loss = finish(own, value, loss)
    return (loss[None], item_grad)


def solution(mesh):
    in_specs = (
        P("wide", "narrow", None, None),
        P("wide", "narrow", None),
        P(),
        P(),
        P(("wide", "narrow"), None),
        P("wide", None),
        P("wide", None, None),
    )
    out_specs = (P("wide", "narrow", None), P(("wide", "narrow"), None))
    return jax.shard_map(local, mesh=mesh, in_specs=in_specs, out_specs=out_specs, check_vma=False)
```

```python
import math

import jax
import jax.numpy as jnp
from jax import lax
from jax.experimental import pallas as pl
from jax.experimental.pallas import tpu as pltpu
from jax.sharding import PartitionSpec as P

D = 256
DH = 128
BLOCK = 128
GROUP = 16
SIDE = 4
SLOTS = 1024
TILE = 256
TILES = SLOTS // TILE
PART = TILE // GROUP
PAIR = SLOTS // GROUP
TOK = 512
CAND = 512
SCALE = 20.0
EARLY = 2
ARRIVE = ((1, 0), (3, 0), (1, 1), (3, 1), (2, 0), (2, 1))
HALF = TOK // 2
FAR_FIRST = (8, 9, 7, 10, 6, 11, 5, 12, 4, 13, 3, 14, 2, 15, 1)
NEAR_FIRST = FAR_FIRST[::-1]
MESH = pl.DeviceIdType.MESH
F32 = jnp.float32
BF16 = jnp.bfloat16


def unit_scale(rows):
    return lax.rsqrt(jnp.mean(rows * rows, axis=-1, keepdims=True) + 1e-06)


def silu(x):
    half = 0.5 * x
    return half + half * jnp.tanh(half)


def main_kernel(
    len_hbm,
    neg_hbm,
    hist_hbm,
    win_hbm,
    wout_hbm,
    table_hbm,
    targets_hbm,
    value_hbm,
    loss_hbm,
    own_hbm,
    len_ref,
    neg_ref,
    hist_ref,
    win_ref,
    wout_ref,
    table_ref,
    targets_ref,
    proj,
    enc,
    tot,
    own_ref,
    units,
    send,
    recv,
    tok,
    cand,
    expd,
    sums,
    gsend,
    grecv,
    hits,
    grad_ref,
    raw_ref,
    begin_ref,
    loss_ref,
    out_s,
    in_s,
    tot_s,
    tot_r,
    a2a_s,
    a2a_r,
    cand_s,
    cand_r,
    tok_s,
    tok_r,
    sum_s,
    sum_r,
    hit_s,
    hit_r,
    g_s,
    g_r,
):
    me = lax.axis_index("wide")
    narrow = lax.axis_index("narrow")
    core = lax.rem(me, 2)
    tok_step = 4 - 3 * core
    cand_step = 1 + 3 * core
    my_t = lax.rem(narrow // tok_step, SIDE)
    my_c = lax.rem(narrow // cand_step, SIDE)

    def wide_peer(d):
        return (lax.rem(me + d, GROUP), narrow)

    def tok_peer(s):
        return (me, lax.rem(my_t + s, SIDE) * tok_step + my_c * cand_step)

    def cand_peer(s):
        return (me, my_t * tok_step + lax.rem(my_c + s, SIDE) * cand_step)

    def remote(src, dst, ssem, rsem, peer):
        return pltpu.make_async_remote_copy(
            src_ref=src, dst_ref=dst, send_sem=ssem, recv_sem=rsem, device_id=peer, device_id_type=MESH
        )

    barrier = pltpu.get_barrier_semaphore()
    for d in FAR_FIRST:
        pl.semaphore_signal(barrier, inc=1, device_id=wide_peer(d), device_id_type=MESH)
    for s in range(1, SIDE):
        pl.semaphore_signal(barrier, inc=1, device_id=tok_peer(s), device_id_type=MESH)
        pl.semaphore_signal(barrier, inc=1, device_id=cand_peer(s), device_id_type=MESH)

    loads = [
        pltpu.make_async_copy(src, dst, in_s.at[i])
        for i, (src, dst) in enumerate(
            [
                (len_hbm, len_ref),
                (neg_hbm, neg_ref),
                (hist_hbm, hist_ref),
                (win_hbm, win_ref),
                (wout_hbm, wout_ref),
                (table_hbm, table_ref),
                (targets_hbm, targets_ref),
            ]
        )
    ]
    for load in loads:
        load.start()
    load_len, load_neg, load_hist, load_win, load_wout, load_table, load_targets = loads

    load_len.wait()
    e0 = len_ref[0, 0, 0]
    e1 = e0 + len_ref[0, 0, 1]
    e2 = e1 + len_ref[0, 0, 2]
    e3 = e2 + len_ref[0, 0, 3]
    tot[me] = jnp.full((8, 128), e3, jnp.int32)

    load_hist.wait()
    load_win.wait()
    for b in range(TILES):
        rows = pl.ds(b * TILE, TILE)
        x = jnp.dot(hist_ref[0, 0, rows, :], win_ref[...], preferred_element_type=F32)
        proj[rows, :] = silu(x).astype(BF16)

    load_neg.wait()
    my_dev = me * GROUP + narrow
    blocks = [neg_ref[narrow * 4 + q] for q in range(4)]
    row8 = lax.broadcasted_iota(jnp.int32, (8, TOK), 0)
    row8s = row8[:, :128]
    half_of = lax.broadcasted_iota(jnp.int32, (8, TOK), 1) >> 8
    held = jnp.zeros((8, 128), jnp.int32)
    for q in range(4):
        held = jnp.where(row8s == q, blocks[q], held)
    own_ref[...] = held * BLOCK
    load_table.wait()
    own = [jnp.full((16, D), blocks[q] - my_dev * 16, jnp.int32) for q in range(4)]

    @pl.loop(0, BLOCK // 16)
    def _(i):
        at = pl.multiple_of(i * 16, 16)
        picked = [jnp.zeros((16, D), F32)] * 4
        for b in range(16):
            rows = table_ref[pl.ds(b * BLOCK + at, 16), :]
            picked = [jnp.where(own[q] == b, rows, picked[q]) for q in range(4)]
        for q in range(4):
            raw_ref[pl.ds(q * BLOCK + at, 16), :] = picked[q]

    rows = raw_ref[...]
    units[...] = (rows * unit_scale(rows) * 0.0625).astype(BF16)
    cand[my_c] = units[...]

    lanes = lax.broadcasted_iota(jnp.int32, (TILE, TILE), 1)
    subs = lax.broadcasted_iota(jnp.int32, (TILE, TILE), 0)
    load_wout.wait()

    def encode(b):
        rows = pl.ds(b * TILE, TILE)
        place = subs + b * TILE
        start = jnp.maximum(
            jnp.maximum(jnp.where(place >= e0, e0, 0), jnp.where(place >= e1, e1, 0)),
            jnp.maximum(jnp.where(place >= e2, e2, 0), jnp.where(place >= e3, e3, 0)),
        )
        share = 1.0 / (place - start + 1).astype(F32)
        heads = []
        for h in range(2):
            q = proj[rows, pl.ds(512 + h * DH, DH)]
            total = jnp.zeros((TILE, DH), F32)
            for kb in range(b + 1):
                krows = pl.ds(kb * TILE, TILE)
                k = proj[krows, pl.ds(768 + h * DH, DH)]
                v = proj[krows, pl.ds(256 + h * DH, DH)]
                scores = lax.dot_general(q, k, (((1,), (1,)), ((), ())), preferred_element_type=F32)
                weights = silu(scores * (DH ** -0.5)) * share
                allowed = lanes + kb * TILE >= start
                if kb == b:
                    allowed = allowed & (lanes <= subs)
                weights = jnp.where(allowed, weights, 0.0).astype(BF16)
                total = total + jnp.dot(weights, v, preferred_element_type=F32)
            heads.append(total)
        attended = jnp.concatenate(heads, axis=1)
        centred = attended - jnp.mean(attended, axis=-1, keepdims=True)
        spread = jnp.mean(centred * centred, axis=-1, keepdims=True)
        gate = proj[rows, pl.ds(0, D)].astype(F32)
        mixed = (centred * lax.rsqrt(spread + 1e-05) * gate).astype(BF16)
        state = hist_ref[0, 0, rows, :].astype(F32) + jnp.dot(mixed, wout_ref[...], preferred_element_type=F32)
        enc[rows, :] = jnp.where(place < e3, state * unit_scale(state) * 0.0625, 0.0).astype(BF16)

    for b in range(EARLY):
        encode(b)

    pl.semaphore_wait(barrier, GROUP - 1 + 2 * (SIDE - 1))
    tot_copies = [remote(tot.at[me], tot.at[me], tot_s.at[d], tot_r.at[d], wide_peer(d)) for d in FAR_FIRST]
    cand_copies = [
        remote(units, cand.at[my_c], cand_s.at[s], cand_r.at[s], cand_peer(s)) for s in range(1, SIDE)
    ]
    for copy in tot_copies + cand_copies:
        copy.start()

    for b in range(EARLY, TILES):
        encode(b)

    low = me < GROUP // 2
    begin_ref[...] = jnp.where(low, 0, -e3) + jnp.zeros((8, 128), jnp.int32)

    def near(d):
        w = lax.rem(me + GROUP - d, GROUP)
        return (low & (w < me)) | (jnp.logical_not(low) & (w > me))

    for d, copy in zip(NEAR_FIRST, tot_copies[::-1]):

        @pl.when(near(d))
        def _():
            copy.wait_recv()
            other = tot[lax.rem(me + GROUP - d, GROUP)]
            begin_ref[...] += jnp.where(low, other, -other)

    begin = begin_ref[...]
    begin = jnp.concatenate([begin[0:1, :]] * 2, axis=1)
    wanted = (subs & 15) * 16 + (((subs >> 4) - begin) & 15)
    take = (lanes == wanted).astype(F32).astype(BF16)
    for b in range(TILES):
        packed = jnp.dot(take, enc[pl.ds(b * TILE, TILE), :], preferred_element_type=F32).astype(BF16)
        send[:, pl.ds(b * PART, PART), :] = packed.reshape(GROUP, PART, D)
    for d in FAR_FIRST:
        dest = lax.rem(me + d, GROUP)
        remote(send.at[dest], recv.at[me], a2a_s, a2a_r, wide_peer(d)).start()
    recv[me] = send[me]

    for d, copy in zip(NEAR_FIRST, tot_copies[::-1]):
        pl.when(jnp.logical_not(near(d)))(copy.wait_recv)
    lane = lax.broadcasted_iota(jnp.int32, (1, 128), 1)
    slot = lax.broadcasted_iota(jnp.int32, (TOK, 128), 0)
    begin = jnp.zeros((1, 128), jnp.int32)
    pieces = []
    for w in range(0, GROUP, 2):
        second = begin + tot[w, 0:1, :]
        base = jnp.where(lane < PAIR, begin, second)
        goes_to = ((base - me + 15) >> 4) + (lane & (PAIR - 1))
        pieces.append((slot == goes_to).astype(F32).astype(BF16))
        begin = second + tot[w + 1, 0:1, :]
    gather = jnp.concatenate(pieces, axis=1)
    pltpu.make_async_copy(recv.at[pl.ds(0, GROUP - 1)], recv.at[pl.ds(0, GROUP - 1)], a2a_r).wait()
    own_tok = jnp.dot(gather, recv[...].reshape(GROUP * PAIR, D), preferred_element_type=F32).astype(BF16)
    tok[2 * my_t] = own_tok[:HALF]
    tok[2 * my_t + 1] = own_tok[HALF:]

    tok_copies = {
        (s, h): remote(
            tok.at[2 * my_t + h], tok.at[2 * my_t + h], tok_s.at[2 * s + h], tok_r.at[2 * s + h], tok_peer(s)
        )
        for s, h in ARRIVE
    }
    for key in ARRIVE:
        tok_copies[key].start()
    for copy in cand_copies:
        copy.wait_recv()

    part = jnp.zeros((8, TOK), F32)
    for s, h in ((0, 0), (0, 1)) + ARRIVE:
        if s:
            tok_copies[s, h].wait_recv()
        t = lax.rem(my_t + SIDE - s, SIDE)

        def forward(c, total):
            scores = lax.dot_general(
                cand[c], tok[2 * t + h], (((1,), (1,)), ((), ())), preferred_element_type=F32
            )
            value = jnp.exp2(scores * (SCALE * math.log2(math.e)))
            expd[t, pl.ds(pl.multiple_of(c * CAND, CAND), CAND), pl.ds(h * HALF, HALF)] = value
            return total + jnp.sum(value.reshape(CAND // 8, 8, TOK // 2), axis=0)

        total = lax.fori_loop(0, SIDE, forward, jnp.zeros((8, TOK // 2), F32))
        total = jnp.concatenate([jnp.sum(total, axis=0, keepdims=True)] * 2, axis=1)
        part = jnp.where((row8 == t) & (half_of == h), total, part)
    sums[my_t] = part
    sum_copies = [
        remote(sums.at[my_t], sums.at[my_t], sum_s.at[s], sum_r.at[s], tok_peer(s)) for s in range(1, SIDE)
    ]
    for s in (2, 1, 3):
        sum_copies[s - 1].start()

    load_targets.wait()
    offset = lax.broadcasted_iota(jnp.int32, (BLOCK, TOK), 0)

    def block_start(c, q):
        return neg_ref[(my_t * tok_step + c * cand_step) * 4 + q] * BLOCK

    def target_of(t):
        return targets_ref[0, pl.ds(t * tok_step + my_c * cand_step, 1), :]

    for copy in sum_copies:
        copy.wait_recv()
    sumexp = (sums[0] + sums[1]) + (sums[2] + sums[3])
    inverse = 1.0 / sumexp

    g_copies = []
    part = jnp.zeros((8, TOK), F32)
    for s in (2, 1, 3, 0):
        c = lax.rem(my_c + s, SIDE)
        for half in range(2):
            total = jnp.zeros((2 * BLOCK, D), F32)
            for t in range(SIDE):
                target = target_of(t)
                scale_t = inverse[t : t + 1, :]
                slopes = []
                found = jnp.zeros((8, TOK), F32)
                for q in (2 * half, 2 * half + 1):
                    value = expd[t, pl.ds(pl.multiple_of(c * CAND + q * BLOCK, BLOCK), BLOCK), :]
                    hit = offset == target - block_start(c, q)
                    slopes.append((value * scale_t - jnp.where(hit, 1.0, 0.0)).astype(BF16))
                    found = found + jnp.sum(jnp.where(hit, value, 0.0).reshape(BLOCK // 8, 8, TOK), axis=0)
                total = total + jnp.dot(jnp.concatenate(slopes, axis=0), tok[2 * t : 2 * t + 2].reshape(TOK, D), preferred_element_type=F32)
                part = part + jnp.where(row8 == t, jnp.sum(found, axis=0, keepdims=True), 0.0)
            rows = pl.ds(half * 2 * BLOCK, 2 * BLOCK)
            if s:
                gsend[2 * s + half] = (SCALE * total).astype(BF16)
                copy = remote(
                    gsend.at[2 * s + half],
                    grecv.at[2 * s + half],
                    g_s.at[2 * s + half],
                    g_r.at[2 * s + half],
                    cand_peer(s),
                )
                copy.start()
                g_copies.append(copy)
            else:
                grad_ref[rows, :] = SCALE * total
    hits[my_t] = part
    hit_copies = [
        remote(hits.at[my_t], hits.at[my_t], hit_s.at[s], hit_r.at[s], tok_peer(s)) for s in range(1, SIDE)
    ]
    for s in (2, 1, 3):
        hit_copies[s - 1].start()
    for copy in hit_copies:
        copy.wait_recv()
    found = (hits[0] + hits[1]) + (hits[2] + hits[3])
    loss = jnp.where(row8 == my_t, jnp.log(sumexp) - jnp.log(found), 0.0)
    loss_ref[...] = jnp.sum(loss, axis=0, keepdims=True)
    outs = [
        pltpu.make_async_copy(loss_ref, loss_hbm, out_s.at[1]),
        pltpu.make_async_copy(own_ref, own_hbm, out_s.at[2]),
    ]
    for copy in outs:
        copy.start()
    for q in range(4):
        if q % 2 == 0:
            for s in range(3):
                g_copies[2 * s + q // 2].wait_recv()
        at = pl.ds(q * BLOCK, BLOCK)
        part = pl.ds(q % 2 * BLOCK, BLOCK)
        grad = (grad_ref[at, :] + grecv[2 + q // 2, part, :].astype(F32)) + (
            grecv[4 + q // 2, part, :].astype(F32) + grecv[6 + q // 2, part, :].astype(F32)
        )
        rows = raw_ref[at, :]
        scale = unit_scale(rows)
        along = jnp.mean(rows * grad, axis=-1, keepdims=True)
        grad_ref[at, :] = (grad - rows * (scale * scale * along)) * (scale * 0.0625)
    outs.append(pltpu.make_async_copy(grad_ref, value_hbm, out_s.at[0]))
    outs[-1].start()

    for copy in tot_copies + cand_copies + list(tok_copies.values()) + sum_copies + hit_copies + g_copies:
        copy.wait_send()
    for copy in outs:
        copy.wait()
    pltpu.make_async_copy(recv.at[pl.ds(0, GROUP - 1)], recv.at[pl.ds(0, GROUP - 1)], a2a_s).wait()


def main(lengths, neg_blocks, histories, w_in, w_out, item_table, targets):
    dma = pltpu.SemaphoreType.DMA
    anywhere = pl.BlockSpec(memory_space=pl.ANY)
    return pl.pallas_call(
        main_kernel,
        out_shape=(
            jax.ShapeDtypeStruct((CAND, D), F32),
            jax.ShapeDtypeStruct((1, TOK), F32),
            jax.ShapeDtypeStruct((8, 128), jnp.int32),
        ),
        in_specs=[anywhere] * 7,
        out_specs=(anywhere, anywhere, anywhere),
        scratch_shapes=[
            pltpu.SMEM((1, 1, 4), jnp.int32),
            pltpu.SMEM((64,), jnp.int32),
            pltpu.VMEM((1, 1, SLOTS, D), BF16),
            pltpu.VMEM((D, 4 * D), BF16),
            pltpu.VMEM((D, D), BF16),
            pltpu.VMEM((16 * BLOCK, D), F32),
            pltpu.VMEM((1, GROUP, TOK), jnp.int32),
            pltpu.VMEM((SLOTS, 4 * D), BF16),
            pltpu.VMEM((SLOTS, D), BF16),
            pltpu.VMEM((GROUP, 8, 128), jnp.int32),
            pltpu.VMEM((8, 128), jnp.int32),
            pltpu.VMEM((CAND, D), BF16),
            pltpu.VMEM((GROUP, PAIR, D), BF16),
            pltpu.VMEM((GROUP, PAIR, D), BF16),
            pltpu.VMEM((2 * SIDE, HALF, D), BF16),
            pltpu.VMEM((SIDE, CAND, D), BF16),
            pltpu.VMEM((SIDE, SIDE * CAND, TOK), F32),
            pltpu.VMEM((SIDE, 8, TOK), F32),
            pltpu.VMEM((2 * SIDE, HALF, D), BF16),
            pltpu.VMEM((2 * SIDE, HALF, D), BF16),
            pltpu.VMEM((SIDE, 8, TOK), F32),
            pltpu.VMEM((CAND, D), F32),
            pltpu.VMEM((CAND, D), F32),
            pltpu.VMEM((8, 128), jnp.int32),
            pltpu.VMEM((1, TOK), F32),
            dma((3,)),
            dma((7,)),
            dma((GROUP,)),
            dma((GROUP,)),
            dma,
            dma,
        ]
        + [dma((SIDE,))] * 2
        + [dma((2 * SIDE,))] * 2
        + [dma((SIDE,))] * 4
        + [dma((2 * SIDE,))] * 2,
        compiler_params=pltpu.CompilerParams(
            collective_id=0, has_side_effects=True, vmem_limit_bytes=56 * 2**20
        ),
        name="main",
    )(lengths, neg_blocks, histories, w_in, w_out, item_table, targets)


def finish_kernel(own_hbm, value_hbm, loss_in, out_hbm, loss_hbm, zeros, value_ref, loss_ref, own_ref, in_s, out_s):
    first = (lax.axis_index("wide") * GROUP + lax.axis_index("narrow")) * 16 * BLOCK
    loads = [
        pltpu.make_async_copy(own_hbm, own_ref, in_s.at[0]),
        pltpu.make_async_copy(loss_in, loss_ref, in_s.at[1]),
        pltpu.make_async_copy(value_hbm, value_ref, in_s.at[2]),
    ]
    for load in loads:
        load.start()
    zeros[...] = jnp.zeros_like(zeros)
    blanks = [
        pltpu.make_async_copy(zeros, out_hbm.at[pl.ds(i * CAND, CAND)], out_s.at[i]) for i in range(4)
    ]
    for blank in blanks:
        blank.start()
    loads[1].wait()
    moves = [pltpu.make_async_copy(loss_ref, loss_hbm, out_s.at[8])]
    moves[0].start()
    loads[0].wait()
    loads[2].wait()
    for blank in blanks:
        blank.wait()
    for q in range(4):
        at = pl.multiple_of(own_ref[q, 0] - first, BLOCK)
        moves.append(
            pltpu.make_async_copy(
                value_ref.at[pl.ds(q * BLOCK, BLOCK)], out_hbm.at[pl.ds(at, BLOCK)], out_s.at[4 + q]
            )
        )
        moves[-1].start()
    for move in moves:
        move.wait()


def finish(own, value, loss):
    anywhere = pl.BlockSpec(memory_space=pl.ANY)
    return pl.pallas_call(
        finish_kernel,
        out_shape=(jax.ShapeDtypeStruct((16 * BLOCK, D), F32), jax.ShapeDtypeStruct((1, TOK), F32)),
        in_specs=[anywhere] * 3,
        out_specs=(anywhere, anywhere),
        scratch_shapes=[
            pltpu.VMEM((CAND, D), F32),
            pltpu.VMEM((CAND, D), F32),
            pltpu.VMEM((1, TOK), F32),
            pltpu.SMEM((8, 128), jnp.int32),
            pltpu.SemaphoreType.DMA((3,)),
            pltpu.SemaphoreType.DMA((9,)),
        ],
        compiler_params=pltpu.CompilerParams(vmem_limit_bytes=56 * 2**20),
        name="finish",
    )(own, value, loss)


def local(histories, lengths, w_in, w_out, item_table, neg_blocks, targets):
    blocks = neg_blocks[0]
    rank = jnp.sum((blocks[None, :] < blocks[:, None]).astype(jnp.int32), axis=1)
    places = jnp.arange(blocks.shape[0], dtype=jnp.int32)
    order = jnp.sum(jnp.where(rank[:, None] == places[None, :], blocks[:, None], 0), axis=0)
    value, loss, own = main(lengths, order, histories, w_in, w_out, item_table, targets)
    item_grad, loss = finish(own, value, loss)
    return (loss[None], item_grad)


def solution(mesh):
    in_specs = (
        P("wide", "narrow", None, None),
        P("wide", "narrow", None),
        P(),
        P(),
        P(("wide", "narrow"), None),
        P("wide", None),
        P("wide", None, None),
    )
    out_specs = (P("wide", "narrow", None), P(("wide", "narrow"), None))
    return jax.shard_map(local, mesh=mesh, in_specs=in_specs, out_specs=out_specs, check_vma=False)
```

```python
import math

import jax
import jax.numpy as jnp
from jax import lax
from jax.experimental import pallas as pl
from jax.experimental.pallas import tpu as pltpu
from jax.sharding import PartitionSpec as P

D = 256
DH = 128
BLOCK = 128
GROUP = 16
SIDE = 4
SLOTS = 1024
TILE = 256
TILES = SLOTS // TILE
PART = TILE // GROUP
PAIR = SLOTS // GROUP
TOK = 512
CAND = 512
SCALE = 20.0
EARLY = 1
ARRIVE = ((1, 0), (3, 0), (1, 1), (3, 1), (2, 0), (2, 1))
HALF = TOK // 2
FAR_FIRST = (8, 9, 7, 10, 6, 11, 5, 12, 4, 13, 3, 14, 2, 15, 1)
NEAR_FIRST = FAR_FIRST[::-1]
MESH = pl.DeviceIdType.MESH
F32 = jnp.float32
BF16 = jnp.bfloat16


def unit_scale(rows):
    return lax.rsqrt(jnp.mean(rows * rows, axis=-1, keepdims=True) + 1e-06)


def silu(x):
    half = 0.5 * x
    return half + half * jnp.tanh(half)


def main_kernel(
    len_hbm,
    neg_hbm,
    hist_hbm,
    win_hbm,
    wout_hbm,
    table_hbm,
    targets_hbm,
    value_hbm,
    loss_hbm,
    own_hbm,
    len_ref,
    neg_ref,
    hist_ref,
    win_ref,
    wout_ref,
    table_ref,
    targets_ref,
    proj,
    enc,
    tot,
    own_ref,
    units,
    send,
    recv,
    tok,
    cand,
    expd,
    sums,
    gsend,
    grecv,
    hits,
    grad_ref,
    raw_ref,
    begin_ref,
    loss_ref,
    out_s,
    in_s,
    tot_s,
    tot_r,
    a2a_s,
    a2a_r,
    cand_s,
    cand_r,
    tok_s,
    tok_r,
    sum_s,
    sum_r,
    hit_s,
    hit_r,
    g_s,
    g_r,
):
    me = lax.axis_index("wide")
    narrow = lax.axis_index("narrow")
    core = lax.rem(me, 2)
    tok_step = 4 - 3 * core
    cand_step = 1 + 3 * core
    my_t = lax.rem(narrow // tok_step, SIDE)
    my_c = lax.rem(narrow // cand_step, SIDE)

    def wide_peer(d):
        return (lax.rem(me + d, GROUP), narrow)

    def tok_peer(s):
        return (me, lax.rem(my_t + s, SIDE) * tok_step + my_c * cand_step)

    def cand_peer(s):
        return (me, my_t * tok_step + lax.rem(my_c + s, SIDE) * cand_step)

    def remote(src, dst, ssem, rsem, peer):
        return pltpu.make_async_remote_copy(
            src_ref=src, dst_ref=dst, send_sem=ssem, recv_sem=rsem, device_id=peer, device_id_type=MESH
        )

    barrier = pltpu.get_barrier_semaphore()
    for d in FAR_FIRST:
        pl.semaphore_signal(barrier, inc=1, device_id=wide_peer(d), device_id_type=MESH)
    for s in range(1, SIDE):
        pl.semaphore_signal(barrier, inc=1, device_id=tok_peer(s), device_id_type=MESH)
        pl.semaphore_signal(barrier, inc=1, device_id=cand_peer(s), device_id_type=MESH)

    loads = [
        pltpu.make_async_copy(src, dst, in_s.at[i])
        for i, (src, dst) in enumerate(
            [
                (len_hbm, len_ref),
                (neg_hbm, neg_ref),
                (hist_hbm, hist_ref),
                (win_hbm, win_ref),
                (wout_hbm, wout_ref),
                (table_hbm, table_ref),
                (targets_hbm, targets_ref),
            ]
        )
    ]
    for load in loads:
        load.start()
    load_len, load_neg, load_hist, load_win, load_wout, load_table, load_targets = loads

    load_len.wait()
    e0 = len_ref[0, 0, 0]
    e1 = e0 + len_ref[0, 0, 1]
    e2 = e1 + len_ref[0, 0, 2]
    e3 = e2 + len_ref[0, 0, 3]
    tot[me] = jnp.full((8, 128), e3, jnp.int32)

    load_hist.wait()
    load_win.wait()
    for b in range(TILES):
        rows = pl.ds(b * TILE, TILE)
        x = jnp.dot(hist_ref[0, 0, rows, :], win_ref[...], preferred_element_type=F32)
        proj[rows, :] = silu(x).astype(BF16)

    lanes = lax.broadcasted_iota(jnp.int32, (TILE, TILE), 1)
    subs = lax.broadcasted_iota(jnp.int32, (TILE, TILE), 0)
    load_wout.wait()

    def encode(b):
        rows = pl.ds(b * TILE, TILE)
        place = subs + b * TILE
        start = jnp.maximum(
            jnp.maximum(jnp.where(place >= e0, e0, 0), jnp.where(place >= e1, e1, 0)),
            jnp.maximum(jnp.where(place >= e2, e2, 0), jnp.where(place >= e3, e3, 0)),
        )
        share = 1.0 / (place - start + 1).astype(F32)
        heads = []
        for h in range(2):
            q = proj[rows, pl.ds(512 + h * DH, DH)]
            total = jnp.zeros((TILE, DH), F32)
            for kb in range(b + 1):
                krows = pl.ds(kb * TILE, TILE)
                k = proj[krows, pl.ds(768 + h * DH, DH)]
                v = proj[krows, pl.ds(256 + h * DH, DH)]
                scores = lax.dot_general(q, k, (((1,), (1,)), ((), ())), preferred_element_type=F32)
                weights = silu(scores * (DH ** -0.5)) * share
                allowed = lanes + kb * TILE >= start
                if kb == b:
                    allowed = allowed & (lanes <= subs)
                weights = jnp.where(allowed, weights, 0.0).astype(BF16)
                total = total + jnp.dot(weights, v, preferred_element_type=F32)
            heads.append(total)
        attended = jnp.concatenate(heads, axis=1)
        centred = attended - jnp.mean(attended, axis=-1, keepdims=True)
        spread = jnp.mean(centred * centred, axis=-1, keepdims=True)
        gate = proj[rows, pl.ds(0, D)].astype(F32)
        mixed = (centred * lax.rsqrt(spread + 1e-05) * gate).astype(BF16)
        state = hist_ref[0, 0, rows, :].astype(F32) + jnp.dot(mixed, wout_ref[...], preferred_element_type=F32)
        enc[rows, :] = jnp.where(place < e3, state * unit_scale(state) * 0.0625, 0.0).astype(BF16)

    for b in range(EARLY):
        encode(b)

    pl.semaphore_wait(barrier, GROUP - 1 + 2 * (SIDE - 1))
    tot_copies = [remote(tot.at[me], tot.at[me], tot_s.at[d], tot_r.at[d], wide_peer(d)) for d in FAR_FIRST]
    for copy in tot_copies:
        copy.start()

    load_neg.wait()
    my_dev = me * GROUP + narrow
    along = lax.broadcasted_iota(jnp.int32, (64, 64), 1)
    down = lax.broadcasted_iota(jnp.int32, (64, 64), 0)
    listed = jnp.broadcast_to(neg_ref[...].astype(F32), (64, 64))
    column = jnp.sum(jnp.where(along == down, listed, 0.0), axis=1, keepdims=True)
    rank = jnp.sum(jnp.where(listed < column, 1.0, 0.0), axis=1, keepdims=True)
    ordered = jnp.sum(jnp.where(along.astype(F32) == rank, column, 0.0), axis=0, keepdims=True)

    def block_at(k):
        return jnp.sum(jnp.where(along[0:1, :] == k, ordered, 0.0), axis=1, keepdims=True).astype(jnp.int32)

    blocks = [block_at(narrow * 4 + q) for q in range(4)]
    row8 = lax.broadcasted_iota(jnp.int32, (8, TOK), 0)
    row8s = row8[:, :128]
    half_of = lax.broadcasted_iota(jnp.int32, (8, TOK), 1) >> 8
    held = jnp.zeros((8, 128), jnp.int32)
    for q in range(4):
        held = jnp.where(row8s == q, blocks[q], held)
    own_ref[...] = held * BLOCK
    load_table.wait()
    own = [jnp.broadcast_to(blocks[q] - my_dev * 16, (16, D)) for q in range(4)]

    @pl.loop(0, BLOCK // 16)
    def _(i):
        at = pl.multiple_of(i * 16, 16)
        picked = [jnp.zeros((16, D), F32)] * 4
        for b in range(16):
            rows = table_ref[pl.ds(b * BLOCK + at, 16), :]
            picked = [jnp.where(own[q] == b, rows, picked[q]) for q in range(4)]
        for q in range(4):
            raw_ref[pl.ds(q * BLOCK + at, 16), :] = picked[q]

    rows = raw_ref[...]
    units[...] = (rows * unit_scale(rows) * 0.0625).astype(BF16)
    cand[my_c] = units[...]
    cand_copies = [
        remote(units, cand.at[my_c], cand_s.at[s], cand_r.at[s], cand_peer(s)) for s in range(1, SIDE)
    ]
    for copy in cand_copies:
        copy.start()

    for b in range(EARLY, TILES):
        encode(b)

    low = me < GROUP // 2
    begin_ref[...] = jnp.where(low, 0, -e3) + jnp.zeros((8, 128), jnp.int32)

    def near(d):
        w = lax.rem(me + GROUP - d, GROUP)
        return (low & (w < me)) | (jnp.logical_not(low) & (w > me))

    for d, copy in zip(NEAR_FIRST, tot_copies[::-1]):

        @pl.when(near(d))
        def _():
            copy.wait_recv()
            other = tot[lax.rem(me + GROUP - d, GROUP)]
            begin_ref[...] += jnp.where(low, other, -other)

    begin = begin_ref[...]
    begin = jnp.concatenate([begin[0:1, :]] * 2, axis=1)
    wanted = (subs & 15) * 16 + (((subs >> 4) - begin) & 15)
    take = (lanes == wanted).astype(F32).astype(BF16)
    for b in range(TILES):
        packed = jnp.dot(take, enc[pl.ds(b * TILE, TILE), :], preferred_element_type=F32).astype(BF16)
        send[:, pl.ds(b * PART, PART), :] = packed.reshape(GROUP, PART, D)
    for d in FAR_FIRST:
        dest = lax.rem(me + d, GROUP)
        remote(send.at[dest], recv.at[me], a2a_s, a2a_r, wide_peer(d)).start()
    recv[me] = send[me]

    for d, copy in zip(NEAR_FIRST, tot_copies[::-1]):
        pl.when(jnp.logical_not(near(d)))(copy.wait_recv)
    lane = lax.broadcasted_iota(jnp.int32, (1, 128), 1)
    slot = lax.broadcasted_iota(jnp.int32, (TOK, 128), 0)
    begin = jnp.zeros((1, 128), jnp.int32)
    pieces = []
    for w in range(0, GROUP, 2):
        second = begin + tot[w, 0:1, :]
        base = jnp.where(lane < PAIR, begin, second)
        goes_to = ((base - me + 15) >> 4) + (lane & (PAIR - 1))
        pieces.append((slot == goes_to).astype(F32).astype(BF16))
        begin = second + tot[w + 1, 0:1, :]
    gather = jnp.concatenate(pieces, axis=1)
    pltpu.make_async_copy(recv.at[pl.ds(0, GROUP - 1)], recv.at[pl.ds(0, GROUP - 1)], a2a_r).wait()
    own_tok = jnp.dot(gather, recv[...].reshape(GROUP * PAIR, D), preferred_element_type=F32).astype(BF16)
    tok[2 * my_t] = own_tok[:HALF]
    tok[2 * my_t + 1] = own_tok[HALF:]

    tok_copies = {
        (s, h): remote(
            tok.at[2 * my_t + h], tok.at[2 * my_t + h], tok_s.at[2 * s + h], tok_r.at[2 * s + h], tok_peer(s)
        )
        for s, h in ARRIVE
    }
    for key in ARRIVE:
        tok_copies[key].start()
    for copy in cand_copies:
        copy.wait_recv()

    part = jnp.zeros((8, TOK), F32)
    for s, h in ((0, 0), (0, 1)) + ARRIVE:
        if s:
            tok_copies[s, h].wait_recv()
        t = lax.rem(my_t + SIDE - s, SIDE)

        def forward(c, total):
            scores = lax.dot_general(
                cand[c], tok[2 * t + h], (((1,), (1,)), ((), ())), preferred_element_type=F32
            )
            value = jnp.exp2(scores * (SCALE * math.log2(math.e)))
            expd[t, pl.ds(pl.multiple_of(c * CAND, CAND), CAND), pl.ds(h * HALF, HALF)] = value
            return total + jnp.sum(value.reshape(CAND // 8, 8, TOK // 2), axis=0)

        total = lax.fori_loop(0, SIDE, forward, jnp.zeros((8, TOK // 2), F32))
        total = jnp.concatenate([jnp.sum(total, axis=0, keepdims=True)] * 2, axis=1)
        part = jnp.where((row8 == t) & (half_of == h), total, part)
    sums[my_t] = part
    sum_copies = [
        remote(sums.at[my_t], sums.at[my_t], sum_s.at[s], sum_r.at[s], tok_peer(s)) for s in range(1, SIDE)
    ]
    for s in (2, 1, 3):
        sum_copies[s - 1].start()

    load_targets.wait()
    offset = lax.broadcasted_iota(jnp.int32, (BLOCK, TOK), 0)

    starts = {}
    for s in range(SIDE):
        owner = my_t * tok_step + lax.rem(my_c + s, SIDE) * cand_step
        for q in range(4):
            starts[s, q] = block_at(owner * 4 + q) * BLOCK

    def target_of(t):
        return targets_ref[0, pl.ds(t * tok_step + my_c * cand_step, 1), :]

    for copy in sum_copies:
        copy.wait_recv()
    sumexp = (sums[0] + sums[1]) + (sums[2] + sums[3])
    inverse = 1.0 / sumexp

    g_copies = []
    part = jnp.zeros((8, TOK), F32)
    for s in (2, 1, 3, 0):
        c = lax.rem(my_c + s, SIDE)
        for half in range(2):
            total = jnp.zeros((2 * BLOCK, D), F32)
            for t in range(SIDE):
                target = target_of(t)
                scale_t = inverse[t : t + 1, :]
                slopes = []
                found = jnp.zeros((8, TOK), F32)
                for q in (2 * half, 2 * half + 1):
                    value = expd[t, pl.ds(pl.multiple_of(c * CAND + q * BLOCK, BLOCK), BLOCK), :]
                    hit = offset == target - starts[s, q]
                    slopes.append((value * scale_t - jnp.where(hit, 1.0, 0.0)).astype(BF16))
                    found = found + jnp.sum(jnp.where(hit, value, 0.0).reshape(BLOCK // 8, 8, TOK), axis=0)
                total = total + jnp.dot(jnp.concatenate(slopes, axis=0), tok[2 * t : 2 * t + 2].reshape(TOK, D), preferred_element_type=F32)
                part = part + jnp.where(row8 == t, jnp.sum(found, axis=0, keepdims=True), 0.0)
            rows = pl.ds(half * 2 * BLOCK, 2 * BLOCK)
            if s:
                gsend[2 * s + half] = (SCALE * total).astype(BF16)
                copy = remote(
                    gsend.at[2 * s + half],
                    grecv.at[2 * s + half],
                    g_s.at[2 * s + half],
                    g_r.at[2 * s + half],
                    cand_peer(s),
                )
                copy.start()
                g_copies.append(copy)
            else:
                grad_ref[rows, :] = SCALE * total
    hits[my_t] = part
    hit_copies = [
        remote(hits.at[my_t], hits.at[my_t], hit_s.at[s], hit_r.at[s], tok_peer(s)) for s in range(1, SIDE)
    ]
    for s in (2, 1, 3):
        hit_copies[s - 1].start()
    for copy in hit_copies:
        copy.wait_recv()
    found = (hits[0] + hits[1]) + (hits[2] + hits[3])
    loss = jnp.where(row8 == my_t, jnp.log(sumexp) - jnp.log(found), 0.0)
    loss_ref[...] = jnp.sum(loss, axis=0, keepdims=True)
    outs = [
        pltpu.make_async_copy(loss_ref, loss_hbm, out_s.at[1]),
        pltpu.make_async_copy(own_ref, own_hbm, out_s.at[2]),
    ]
    for copy in outs:
        copy.start()
    for q in range(4):
        if q % 2 == 0:
            for s in range(3):
                g_copies[2 * s + q // 2].wait_recv()
        at = pl.ds(q * BLOCK, BLOCK)
        part = pl.ds(q % 2 * BLOCK, BLOCK)
        grad = (grad_ref[at, :] + grecv[2 + q // 2, part, :].astype(F32)) + (
            grecv[4 + q // 2, part, :].astype(F32) + grecv[6 + q // 2, part, :].astype(F32)
        )
        rows = raw_ref[at, :]
        scale = unit_scale(rows)
        along = jnp.mean(rows * grad, axis=-1, keepdims=True)
        grad_ref[at, :] = (grad - rows * (scale * scale * along)) * (scale * 0.0625)
    outs.append(pltpu.make_async_copy(grad_ref, value_hbm, out_s.at[0]))
    outs[-1].start()

    for copy in tot_copies + cand_copies + list(tok_copies.values()) + sum_copies + hit_copies + g_copies:
        copy.wait_send()
    for copy in outs:
        copy.wait()
    pltpu.make_async_copy(recv.at[pl.ds(0, GROUP - 1)], recv.at[pl.ds(0, GROUP - 1)], a2a_s).wait()


def main(lengths, neg_blocks, histories, w_in, w_out, item_table, targets):
    dma = pltpu.SemaphoreType.DMA
    anywhere = pl.BlockSpec(memory_space=pl.ANY)
    return pl.pallas_call(
        main_kernel,
        out_shape=(
            jax.ShapeDtypeStruct((CAND, D), F32),
            jax.ShapeDtypeStruct((1, TOK), F32),
            jax.ShapeDtypeStruct((8, 128), jnp.int32),
        ),
        in_specs=[anywhere] * 7,
        out_specs=(anywhere, anywhere, anywhere),
        scratch_shapes=[
            pltpu.SMEM((1, 1, 4), jnp.int32),
            pltpu.VMEM((1, 64), jnp.int32),
            pltpu.VMEM((1, 1, SLOTS, D), BF16),
            pltpu.VMEM((D, 4 * D), BF16),
            pltpu.VMEM((D, D), BF16),
            pltpu.VMEM((16 * BLOCK, D), F32),
            pltpu.VMEM((1, GROUP, TOK), jnp.int32),
            pltpu.VMEM((SLOTS, 4 * D), BF16),
            pltpu.VMEM((SLOTS, D), BF16),
            pltpu.VMEM((GROUP, 8, 128), jnp.int32),
            pltpu.VMEM((8, 128), jnp.int32),
            pltpu.VMEM((CAND, D), BF16),
            pltpu.VMEM((GROUP, PAIR, D), BF16),
            pltpu.VMEM((GROUP, PAIR, D), BF16),
            pltpu.VMEM((2 * SIDE, HALF, D), BF16),
            pltpu.VMEM((SIDE, CAND, D), BF16),
            pltpu.VMEM((SIDE, SIDE * CAND, TOK), F32),
            pltpu.VMEM((SIDE, 8, TOK), F32),
            pltpu.VMEM((2 * SIDE, HALF, D), BF16),
            pltpu.VMEM((2 * SIDE, HALF, D), BF16),
            pltpu.VMEM((SIDE, 8, TOK), F32),
            pltpu.VMEM((CAND, D), F32),
            pltpu.VMEM((CAND, D), F32),
            pltpu.VMEM((8, 128), jnp.int32),
            pltpu.VMEM((1, TOK), F32),
            dma((3,)),
            dma((7,)),
            dma((GROUP,)),
            dma((GROUP,)),
            dma,
            dma,
        ]
        + [dma((SIDE,))] * 2
        + [dma((2 * SIDE,))] * 2
        + [dma((SIDE,))] * 4
        + [dma((2 * SIDE,))] * 2,
        compiler_params=pltpu.CompilerParams(
            collective_id=0, has_side_effects=True, vmem_limit_bytes=56 * 2**20
        ),
        name="main",
    )(lengths, neg_blocks, histories, w_in, w_out, item_table, targets)


def finish_kernel(own_hbm, value_hbm, loss_in, out_hbm, loss_hbm, zeros, value_ref, loss_ref, own_ref, in_s, out_s):
    first = (lax.axis_index("wide") * GROUP + lax.axis_index("narrow")) * 16 * BLOCK
    loads = [
        pltpu.make_async_copy(own_hbm, own_ref, in_s.at[0]),
        pltpu.make_async_copy(loss_in, loss_ref, in_s.at[1]),
        pltpu.make_async_copy(value_hbm, value_ref, in_s.at[2]),
    ]
    for load in loads:
        load.start()
    zeros[...] = jnp.zeros_like(zeros)
    blanks = [
        pltpu.make_async_copy(zeros, out_hbm.at[pl.ds(i * CAND, CAND)], out_s.at[i]) for i in range(4)
    ]
    for blank in blanks:
        blank.start()
    loads[1].wait()
    moves = [pltpu.make_async_copy(loss_ref, loss_hbm, out_s.at[8])]
    moves[0].start()
    loads[0].wait()
    loads[2].wait()
    for blank in blanks:
        blank.wait()
    for q in range(4):
        at = pl.multiple_of(own_ref[q, 0] - first, BLOCK)
        moves.append(
            pltpu.make_async_copy(
                value_ref.at[pl.ds(q * BLOCK, BLOCK)], out_hbm.at[pl.ds(at, BLOCK)], out_s.at[4 + q]
            )
        )
        moves[-1].start()
    for move in moves:
        move.wait()


def finish(own, value, loss):
    anywhere = pl.BlockSpec(memory_space=pl.ANY)
    return pl.pallas_call(
        finish_kernel,
        out_shape=(jax.ShapeDtypeStruct((16 * BLOCK, D), F32), jax.ShapeDtypeStruct((1, TOK), F32)),
        in_specs=[anywhere] * 3,
        out_specs=(anywhere, anywhere),
        scratch_shapes=[
            pltpu.VMEM((CAND, D), F32),
            pltpu.VMEM((CAND, D), F32),
            pltpu.VMEM((1, TOK), F32),
            pltpu.SMEM((8, 128), jnp.int32),
            pltpu.SemaphoreType.DMA((3,)),
            pltpu.SemaphoreType.DMA((9,)),
        ],
        compiler_params=pltpu.CompilerParams(vmem_limit_bytes=56 * 2**20),
        name="finish",
    )(own, value, loss)


def local(histories, lengths, w_in, w_out, item_table, neg_blocks, targets):
    value, loss, own = main(lengths, neg_blocks, histories, w_in, w_out, item_table, targets)
    item_grad, loss = finish(own, value, loss)
    return (loss[None], item_grad)


def solution(mesh):
    in_specs = (
        P("wide", "narrow", None, None),
        P("wide", "narrow", None),
        P(),
        P(),
        P(("wide", "narrow"), None),
        P("wide", None),
        P("wide", None, None),
    )
    out_specs = (P("wide", "narrow", None), P(("wide", "narrow"), None))
    return jax.shard_map(local, mesh=mesh, in_specs=in_specs, out_specs=out_specs, check_vma=False)
```

```python
import math

import jax
import jax.numpy as jnp
from jax import lax
from jax.experimental import pallas as pl
from jax.experimental.pallas import tpu as pltpu
from jax.sharding import PartitionSpec as P

D = 256
DH = 128
BLOCK = 128
GROUP = 16
SIDE = 4
SLOTS = 1024
TILE = 256
TILES = SLOTS // TILE
PART = TILE // GROUP
PAIR = SLOTS // GROUP
TOK = 512
CAND = 512
SCALE = 20.0
EARLY = 1
ARRIVE = ((1, 0), (3, 1), (1, 1), (3, 0), (2, 0), (2, 1))
HALF = TOK // 2
FAR_FIRST = (8, 9, 7, 10, 6, 11, 5, 12, 4, 13, 3, 14, 2, 15, 1)
NEAR_FIRST = FAR_FIRST[::-1]
MESH = pl.DeviceIdType.MESH
F32 = jnp.float32
BF16 = jnp.bfloat16


def unit_scale(rows):
    return lax.rsqrt(jnp.mean(rows * rows, axis=-1, keepdims=True) + 1e-06)


def silu(x):
    half = 0.5 * x
    return half + half * jnp.tanh(half)


def main_kernel(
    len_hbm,
    neg_hbm,
    hist_hbm,
    win_hbm,
    wout_hbm,
    table_hbm,
    targets_hbm,
    value_hbm,
    loss_hbm,
    own_hbm,
    len_ref,
    neg_ref,
    hist_ref,
    win_ref,
    wout_ref,
    table_ref,
    targets_ref,
    proj,
    enc,
    tot,
    own_ref,
    units,
    send,
    recv,
    tok,
    cand,
    expd,
    sums,
    gsend,
    grecv,
    hits,
    grad_ref,
    value_ref,
    raw_ref,
    begin_ref,
    loss_ref,
    out_s,
    in_s,
    tot_s,
    tot_r,
    a2a_s,
    a2a_r,
    cand_s,
    cand_r,
    tok_s,
    tok_r,
    sum_s,
    sum_r,
    hit_s,
    hit_r,
    g_s,
    g_r,
):
    me = lax.axis_index("wide")
    narrow = lax.axis_index("narrow")
    core = lax.rem(me, 2)
    tok_step = 4 - 3 * core
    cand_step = 1 + 3 * core
    my_t = lax.rem(narrow // tok_step, SIDE)
    my_c = lax.rem(narrow // cand_step, SIDE)

    def wide_peer(d):
        return (lax.rem(me + d, GROUP), narrow)

    def tok_peer(s):
        return (me, lax.rem(my_t + s, SIDE) * tok_step + my_c * cand_step)

    def cand_peer(s):
        return (me, my_t * tok_step + lax.rem(my_c + s, SIDE) * cand_step)

    def remote(src, dst, ssem, rsem, peer):
        return pltpu.make_async_remote_copy(
            src_ref=src, dst_ref=dst, send_sem=ssem, recv_sem=rsem, device_id=peer, device_id_type=MESH
        )

    barrier = pltpu.get_barrier_semaphore()
    for d in FAR_FIRST:
        pl.semaphore_signal(barrier, inc=1, device_id=wide_peer(d), device_id_type=MESH)
    for s in range(1, SIDE):
        pl.semaphore_signal(barrier, inc=1, device_id=tok_peer(s), device_id_type=MESH)
        pl.semaphore_signal(barrier, inc=1, device_id=cand_peer(s), device_id_type=MESH)

    loads = [
        pltpu.make_async_copy(src, dst, in_s.at[i])
        for i, (src, dst) in enumerate(
            [
                (len_hbm, len_ref),
                (neg_hbm, neg_ref),
                (hist_hbm, hist_ref),
                (win_hbm, win_ref),
                (wout_hbm, wout_ref),
                (table_hbm, table_ref),
                (targets_hbm, targets_ref),
            ]
        )
    ]
    for load in loads:
        load.start()
    load_len, load_neg, load_hist, load_win, load_wout, load_table, load_targets = loads

    load_len.wait()
    e0 = len_ref[0, 0, 0]
    e1 = e0 + len_ref[0, 0, 1]
    e2 = e1 + len_ref[0, 0, 2]
    e3 = e2 + len_ref[0, 0, 3]
    tot[me] = jnp.full((8, 128), e3, jnp.int32)

    load_hist.wait()
    load_win.wait()
    for b in range(TILES):
        rows = pl.ds(b * TILE, TILE)
        x = jnp.dot(hist_ref[0, 0, rows, :], win_ref[...], preferred_element_type=F32)
        proj[rows, :] = silu(x).astype(BF16)

    lanes = lax.broadcasted_iota(jnp.int32, (TILE, TILE), 1)
    subs = lax.broadcasted_iota(jnp.int32, (TILE, TILE), 0)
    load_wout.wait()

    def encode(b):
        rows = pl.ds(b * TILE, TILE)
        place = subs + b * TILE
        start = jnp.maximum(
            jnp.maximum(jnp.where(place >= e0, e0, 0), jnp.where(place >= e1, e1, 0)),
            jnp.maximum(jnp.where(place >= e2, e2, 0), jnp.where(place >= e3, e3, 0)),
        )
        share = 1.0 / (place - start + 1).astype(F32)
        heads = []
        for h in range(2):
            q = proj[rows, pl.ds(512 + h * DH, DH)]
            total = jnp.zeros((TILE, DH), F32)
            for kb in range(b + 1):
                krows = pl.ds(kb * TILE, TILE)
                k = proj[krows, pl.ds(768 + h * DH, DH)]
                v = proj[krows, pl.ds(256 + h * DH, DH)]
                scores = lax.dot_general(q, k, (((1,), (1,)), ((), ())), preferred_element_type=F32)
                weights = silu(scores * (DH ** -0.5)) * share
                allowed = lanes + kb * TILE >= start
                if kb == b:
                    allowed = allowed & (lanes <= subs)
                weights = jnp.where(allowed, weights, 0.0).astype(BF16)
                total = total + jnp.dot(weights, v, preferred_element_type=F32)
            heads.append(total)
        attended = jnp.concatenate(heads, axis=1)
        centred = attended - jnp.mean(attended, axis=-1, keepdims=True)
        spread = jnp.mean(centred * centred, axis=-1, keepdims=True)
        gate = proj[rows, pl.ds(0, D)].astype(F32)
        mixed = (centred * lax.rsqrt(spread + 1e-05) * gate).astype(BF16)
        state = hist_ref[0, 0, rows, :].astype(F32) + jnp.dot(mixed, wout_ref[...], preferred_element_type=F32)
        enc[rows, :] = jnp.where(place < e3, state * unit_scale(state) * 0.0625, 0.0).astype(BF16)

    for b in range(EARLY):
        encode(b)

    pl.semaphore_wait(barrier, GROUP - 1 + 2 * (SIDE - 1))
    tot_copies = [remote(tot.at[me], tot.at[me], tot_s.at[d], tot_r.at[d], wide_peer(d)) for d in FAR_FIRST]
    for copy in tot_copies:
        copy.start()

    load_neg.wait()
    my_dev = me * GROUP + narrow
    along = lax.broadcasted_iota(jnp.int32, (64, 64), 1)
    down = lax.broadcasted_iota(jnp.int32, (64, 64), 0)
    listed = jnp.broadcast_to(neg_ref[...].astype(F32), (64, 64))
    column = jnp.sum(jnp.where(along == down, listed, 0.0), axis=1, keepdims=True)
    rank = jnp.sum(jnp.where(listed < column, 1.0, 0.0), axis=1, keepdims=True)
    ordered = jnp.sum(jnp.where(along.astype(F32) == rank, column, 0.0), axis=0, keepdims=True)

    def block_at(k):
        return jnp.sum(jnp.where(along[0:1, :] == k, ordered, 0.0), axis=1, keepdims=True).astype(jnp.int32)

    blocks = [block_at(narrow * 4 + q) for q in range(4)]
    row8 = lax.broadcasted_iota(jnp.int32, (8, TOK), 0)
    row8s = row8[:, :128]
    half_of = lax.broadcasted_iota(jnp.int32, (8, TOK), 1) >> 8
    held = jnp.zeros((8, 128), jnp.int32)
    for q in range(4):
        held = jnp.where(row8s == q, blocks[q], held)
    own_ref[...] = held * BLOCK
    load_table.wait()
    own = [jnp.broadcast_to(blocks[q] - my_dev * 16, (16, D)) for q in range(4)]

    @pl.loop(0, BLOCK // 16)
    def _(i):
        at = pl.multiple_of(i * 16, 16)
        picked = [jnp.zeros((16, D), F32)] * 4
        for b in range(16):
            rows = table_ref[pl.ds(b * BLOCK + at, 16), :]
            picked = [jnp.where(own[q] == b, rows, picked[q]) for q in range(4)]
        for q in range(4):
            raw_ref[pl.ds(q * BLOCK + at, 16), :] = picked[q]

    rows = raw_ref[...]
    units[...] = (rows * unit_scale(rows) * 0.0625).astype(BF16)
    cand[my_c] = units[...]
    cand_copies = [
        remote(units, cand.at[my_c], cand_s.at[s], cand_r.at[s], cand_peer(s)) for s in range(1, SIDE)
    ]
    for copy in cand_copies:
        copy.start()

    for b in range(EARLY, TILES):
        encode(b)

    low = me < GROUP // 2
    begin_ref[...] = jnp.where(low, 0, -e3) + jnp.zeros((8, 128), jnp.int32)

    def near(d):
        w = lax.rem(me + GROUP - d, GROUP)
        return (low & (w < me)) | (jnp.logical_not(low) & (w > me))

    for d, copy in zip(NEAR_FIRST, tot_copies[::-1]):

        @pl.when(near(d))
        def _():
            copy.wait_recv()
            other = tot[lax.rem(me + GROUP - d, GROUP)]
            begin_ref[...] += jnp.where(low, other, -other)

    begin = begin_ref[...]
    begin = jnp.concatenate([begin[0:1, :]] * 2, axis=1)
    wanted = (subs & 15) * 16 + (((subs >> 4) - begin) & 15)
    take = (lanes == wanted).astype(F32).astype(BF16)
    for b in range(TILES):
        packed = jnp.dot(take, enc[pl.ds(b * TILE, TILE), :], preferred_element_type=F32).astype(BF16)
        send[:, pl.ds(b * PART, PART), :] = packed.reshape(GROUP, PART, D)
    for d in FAR_FIRST:
        dest = lax.rem(me + d, GROUP)
        remote(send.at[dest], recv.at[me], a2a_s, a2a_r, wide_peer(d)).start()
    recv[me] = send[me]

    for d, copy in zip(NEAR_FIRST, tot_copies[::-1]):
        pl.when(jnp.logical_not(near(d)))(copy.wait_recv)
    lane = lax.broadcasted_iota(jnp.int32, (1, 128), 1)
    slot = lax.broadcasted_iota(jnp.int32, (TOK, 128), 0)
    begin = jnp.zeros((1, 128), jnp.int32)
    pieces = []
    for w in range(0, GROUP, 2):
        second = begin + tot[w, 0:1, :]
        base = jnp.where(lane < PAIR, begin, second)
        goes_to = ((base - me + 15) >> 4) + (lane & (PAIR - 1))
        pieces.append((slot == goes_to).astype(F32).astype(BF16))
        begin = second + tot[w + 1, 0:1, :]
    gather = jnp.concatenate(pieces, axis=1)
    pltpu.make_async_copy(recv.at[pl.ds(0, GROUP - 1)], recv.at[pl.ds(0, GROUP - 1)], a2a_r).wait()
    received = recv[...].reshape(GROUP * PAIR, D)
    tok_copies = {}
    for h in (0, 1):
        half = jnp.dot(gather[h * HALF : (h + 1) * HALF], received, preferred_element_type=F32)
        tok[2 * my_t + h] = half.astype(BF16)
        for s in ((1,), (3, 1, 3))[h]:
            part_h = 0 if (s, h) in tok_copies else h
            slot_h = tok.at[2 * my_t + part_h]
            at = 2 * s + part_h
            tok_copies[s, part_h] = remote(slot_h, slot_h, tok_s.at[at], tok_r.at[at], tok_peer(s))
            tok_copies[s, part_h].start()
    for copy in cand_copies:
        copy.wait_recv()

    part = jnp.zeros((8, TOK), F32)
    for s, h in ((0, 0), (0, 1)) + ARRIVE:
        if (s, h) == (1, 0):
            for near_s, near_h in ((1, 0), (3, 1)):
                tok_copies[near_s, near_h].wait_recv()
                slot_h = tok.at[2 * lax.rem(my_t + SIDE - near_s, SIDE) + near_h]
                at = 4 + near_h
                tok_copies[2, near_h] = remote(slot_h, slot_h, tok_s.at[at], tok_r.at[at], tok_peer(near_s))
                tok_copies[2, near_h].start()
        elif s and (s, h) != (3, 1):
            tok_copies[s, h].wait_recv()
        t = lax.rem(my_t + SIDE - s, SIDE)

        def forward(c, total):
            scores = lax.dot_general(
                cand[c], tok[2 * t + h], (((1,), (1,)), ((), ())), preferred_element_type=F32
            )
            value = jnp.exp2(scores * (SCALE * math.log2(math.e)))
            expd[t, pl.ds(pl.multiple_of(c * CAND, CAND), CAND), pl.ds(h * HALF, HALF)] = value
            return total + jnp.sum(value.reshape(CAND // 8, 8, TOK // 2), axis=0)

        total = lax.fori_loop(0, SIDE, forward, jnp.zeros((8, TOK // 2), F32))
        total = jnp.concatenate([jnp.sum(total, axis=0, keepdims=True)] * 2, axis=1)
        part = jnp.where((row8 == t) & (half_of == h), total, part)
    sums[my_t] = part
    sum_copies = [
        remote(sums.at[my_t], sums.at[my_t], sum_s.at[s], sum_r.at[s], tok_peer(s)) for s in range(1, SIDE)
    ]
    for s in (2, 1, 3):
        sum_copies[s - 1].start()

    load_targets.wait()
    offset = lax.broadcasted_iota(jnp.int32, (BLOCK, TOK), 0)

    starts = {}
    for s in range(SIDE):
        owner = my_t * tok_step + lax.rem(my_c + s, SIDE) * cand_step
        for q in range(4):
            starts[s, q] = block_at(owner * 4 + q) * BLOCK

    def target_of(t):
        return targets_ref[0, pl.ds(t * tok_step + my_c * cand_step, 1), :]

    for copy in sum_copies:
        copy.wait_recv()
    sumexp = (sums[0] + sums[1]) + (sums[2] + sums[3])
    inverse = 1.0 / sumexp

    g_copies = {}
    part = jnp.zeros((8, TOK), F32)
    for half, s in ((0, 2), (0, 1), (0, 3), (1, 2), (1, 1), (1, 3), (0, 0), (1, 0)):
        c = lax.rem(my_c + s, SIDE)
        total = jnp.zeros((2 * BLOCK, D), F32)
        for t in range(SIDE):
            target = target_of(t)
            scale_t = inverse[t : t + 1, :]
            slopes = []
            found = jnp.zeros((8, TOK), F32)
            for q in (2 * half, 2 * half + 1):
                value = expd[t, pl.ds(pl.multiple_of(c * CAND + q * BLOCK, BLOCK), BLOCK), :]
                hit = offset == target - starts[s, q]
                slopes.append((value * scale_t - jnp.where(hit, 1.0, 0.0)).astype(BF16))
                found = found + jnp.sum(jnp.where(hit, value, 0.0).reshape(BLOCK // 8, 8, TOK), axis=0)
            both = tok[2 * t : 2 * t + 2].reshape(TOK, D)
            total = total + jnp.dot(jnp.concatenate(slopes, axis=0), both, preferred_element_type=F32)
            part = part + jnp.where(row8 == t, jnp.sum(found, axis=0, keepdims=True), 0.0)
        if s:
            at = 2 * s + half
            gsend[at] = (SCALE * total).astype(BF16)
            copy = remote(gsend.at[at], grecv.at[at], g_s.at[at], g_r.at[at], cand_peer(s))
            copy.start()
            g_copies[s, half] = copy
        else:
            grad_ref[half] = SCALE * total
    hits[my_t] = part
    hit_copies = [
        remote(hits.at[my_t], hits.at[my_t], hit_s.at[s], hit_r.at[s], tok_peer(s)) for s in range(1, SIDE)
    ]
    for s in (2, 1, 3):
        hit_copies[s - 1].start()
    for copy in hit_copies:
        copy.wait_recv()
    found = (hits[0] + hits[1]) + (hits[2] + hits[3])
    loss = jnp.where(row8 == my_t, jnp.log(sumexp) - jnp.log(found), 0.0)
    loss_ref[...] = jnp.sum(loss, axis=0, keepdims=True)
    outs = [
        pltpu.make_async_copy(loss_ref, loss_hbm, out_s.at[1]),
        pltpu.make_async_copy(own_ref, own_hbm, out_s.at[2]),
    ]
    for copy in outs:
        copy.start()
    for half in range(2):
        for s in range(1, SIDE):
            g_copies[s, half].wait_recv()
        grad = (grad_ref[half] + grecv[2 + half].astype(F32)) + (
            grecv[4 + half].astype(F32) + grecv[6 + half].astype(F32)
        )
        at = pl.ds(half * HALF, HALF)
        rows = raw_ref[at, :]
        scale = unit_scale(rows)
        along = jnp.mean(rows * grad, axis=-1, keepdims=True)
        value_ref[half] = (grad - rows * (scale * scale * along)) * (scale * 0.0625)
        outs.append(pltpu.make_async_copy(value_ref.at[half], value_hbm.at[at], out_s.at[3 * half]))
        outs[-1].start()

    for copy in tot_copies + cand_copies + list(tok_copies.values()) + sum_copies + hit_copies + list(g_copies.values()):
        copy.wait_send()
    for copy in outs:
        copy.wait()
    pltpu.make_async_copy(recv.at[pl.ds(0, GROUP - 1)], recv.at[pl.ds(0, GROUP - 1)], a2a_s).wait()


def main(lengths, neg_blocks, histories, w_in, w_out, item_table, targets):
    dma = pltpu.SemaphoreType.DMA
    anywhere = pl.BlockSpec(memory_space=pl.ANY)
    return pl.pallas_call(
        main_kernel,
        out_shape=(
            jax.ShapeDtypeStruct((CAND, D), F32),
            jax.ShapeDtypeStruct((1, TOK), F32),
            jax.ShapeDtypeStruct((8, 128), jnp.int32),
        ),
        in_specs=[anywhere] * 7,
        out_specs=(anywhere, anywhere, anywhere),
        scratch_shapes=[
            pltpu.SMEM((1, 1, 4), jnp.int32),
            pltpu.VMEM((1, 64), jnp.int32),
            pltpu.VMEM((1, 1, SLOTS, D), BF16),
            pltpu.VMEM((D, 4 * D), BF16),
            pltpu.VMEM((D, D), BF16),
            pltpu.VMEM((16 * BLOCK, D), F32),
            pltpu.VMEM((1, GROUP, TOK), jnp.int32),
            pltpu.VMEM((SLOTS, 4 * D), BF16),
            pltpu.VMEM((SLOTS, D), BF16),
            pltpu.VMEM((GROUP, 8, 128), jnp.int32),
            pltpu.VMEM((8, 128), jnp.int32),
            pltpu.VMEM((CAND, D), BF16),
            pltpu.VMEM((GROUP, PAIR, D), BF16),
            pltpu.VMEM((GROUP, PAIR, D), BF16),
            pltpu.VMEM((2 * SIDE, HALF, D), BF16),
            pltpu.VMEM((SIDE, CAND, D), BF16),
            pltpu.VMEM((SIDE, SIDE * CAND, TOK), F32),
            pltpu.VMEM((SIDE, 8, TOK), F32),
            pltpu.VMEM((2 * SIDE, HALF, D), BF16),
            pltpu.VMEM((2 * SIDE, HALF, D), BF16),
            pltpu.VMEM((SIDE, 8, TOK), F32),
            pltpu.VMEM((2, HALF, D), F32),
            pltpu.VMEM((2, HALF, D), F32),
            pltpu.VMEM((CAND, D), F32),
            pltpu.VMEM((8, 128), jnp.int32),
            pltpu.VMEM((1, TOK), F32),
            dma((4,)),
            dma((7,)),
            dma((GROUP,)),
            dma((GROUP,)),
            dma,
            dma,
        ]
        + [dma((SIDE,))] * 2
        + [dma((2 * SIDE,))] * 2
        + [dma((SIDE,))] * 4
        + [dma((2 * SIDE,))] * 2,
        compiler_params=pltpu.CompilerParams(
            collective_id=0, has_side_effects=True, vmem_limit_bytes=56 * 2**20
        ),
        name="main",
    )(lengths, neg_blocks, histories, w_in, w_out, item_table, targets)


def finish_kernel(own_hbm, value_hbm, loss_in, out_hbm, loss_hbm, zeros, value_ref, loss_ref, own_ref, in_s, out_s):
    first = (lax.axis_index("wide") * GROUP + lax.axis_index("narrow")) * 16 * BLOCK
    loads = [
        pltpu.make_async_copy(own_hbm, own_ref, in_s.at[0]),
        pltpu.make_async_copy(loss_in, loss_ref, in_s.at[1]),
        pltpu.make_async_copy(value_hbm, value_ref, in_s.at[2]),
    ]
    for load in loads:
        load.start()
    zeros[...] = jnp.zeros_like(zeros)
    blanks = [
        pltpu.make_async_copy(zeros, out_hbm.at[pl.ds(i * CAND, CAND)], out_s.at[i]) for i in range(4)
    ]
    for blank in blanks:
        blank.start()
    loads[1].wait()
    moves = [pltpu.make_async_copy(loss_ref, loss_hbm, out_s.at[8])]
    moves[0].start()
    loads[0].wait()
    loads[2].wait()
    for blank in blanks:
        blank.wait()
    for q in range(4):
        at = pl.multiple_of(own_ref[q, 0] - first, BLOCK)
        moves.append(
            pltpu.make_async_copy(
                value_ref.at[pl.ds(q * BLOCK, BLOCK)], out_hbm.at[pl.ds(at, BLOCK)], out_s.at[4 + q]
            )
        )
        moves[-1].start()
    for move in moves:
        move.wait()


def finish(own, value, loss):
    anywhere = pl.BlockSpec(memory_space=pl.ANY)
    return pl.pallas_call(
        finish_kernel,
        out_shape=(jax.ShapeDtypeStruct((16 * BLOCK, D), F32), jax.ShapeDtypeStruct((1, TOK), F32)),
        in_specs=[anywhere] * 3,
        out_specs=(anywhere, anywhere),
        scratch_shapes=[
            pltpu.VMEM((CAND, D), F32),
            pltpu.VMEM((CAND, D), F32),
            pltpu.VMEM((1, TOK), F32),
            pltpu.SMEM((8, 128), jnp.int32),
            pltpu.SemaphoreType.DMA((3,)),
            pltpu.SemaphoreType.DMA((9,)),
        ],
        compiler_params=pltpu.CompilerParams(vmem_limit_bytes=56 * 2**20),
        name="finish",
    )(own, value, loss)


def local(histories, lengths, w_in, w_out, item_table, neg_blocks, targets):
    value, loss, own = main(lengths, neg_blocks, histories, w_in, w_out, item_table, targets)
    item_grad, loss = finish(own, value, loss)
    return (loss[None], item_grad)


def solution(mesh):
    in_specs = (
        P("wide", "narrow", None, None),
        P("wide", "narrow", None),
        P(),
        P(),
        P(("wide", "narrow"), None),
        P("wide", None),
        P("wide", None, None),
    )
    out_specs = (P("wide", "narrow", None), P(("wide", "narrow"), None))
    return jax.shard_map(local, mesh=mesh, in_specs=in_specs, out_specs=out_specs, check_vma=False)
```
